128 devices in a mesh: index: 16 (over y, x), query: 8 (over z, core).
Axes of the slice: x: 4, y: 4, z: 4, core: 2. Of those that a mesh axis runs over, the one named last changes fastest.
Arguments:
- queries: bfloat16 [1024, 2048], P(('index', 'query')), may hold values from -4 to 4
- slab: bfloat16 [524288, 2048], P(('index', 'query')), may hold values from -24 to 24
- cand_owner: int32 [1024, 32], P(('index', 'query')), may hold values from 0 to 127, all different within a row; in each aligned block of 8 rows (0 to 7, 8 to 15, ...) at most 4 rows name the same one
- cand_row: int32 [1024, 32], P(('index', 'query')), may hold values from 0 to 4095
Outputs:
- pooled: float32 [1024, 256], P(('index', 'query'))
- coarse_lse: float32 [1024], P(('index', 'query'))
- margin: float32 [1024, 32], P(('index', 'query'))
The draws below stay inside these ranges and needn't reach their ends.
Inputs may be any that keep to these rules, and one draw needn't show every extreme that they name: `cand_owner`: each query names 32 distinct owners. Over the 8 queries of one device (aligned blocks of 8 rows) no owner is named more than 4 times, a bound that some block reaches.
All inputs are finite; a program needn't handle non-finite values.
Results may differ from the reference program's by a relative error of at most 0.00165.
Values may be sent and summed in bfloat16 or wider, within the bound.
A program may use at most 128 MiB of HBM per device.

```python
import math
import jax
import jax.numpy as jnp
import numpy as np
from jax import lax

W = 2048
PREFIX = 256
K = 32
R_DEV = 4096
QD = 8
Q = 1024
ROWS = 524288
CAP = 4
DEVICES = 128


def draw_queries(key, part):
    base = jax.random.normal(jax.random.fold_in(key, 1), (Q, W), jnp.float32)
    return jnp.clip(base, -4.0, 4.0).astype(jnp.bfloat16)


def draw_slab(key, part):
    noise = jnp.clip(jax.random.normal(jax.random.fold_in(key, 2), (ROWS, W), jnp.float32), -4.0, 4.0)
    ramp = 0.75 + 0.5 * jnp.arange(ROWS, dtype=jnp.float32) / ROWS
    row_scale = jnp.exp(jax.random.uniform(jax.random.fold_in(key, 3), (ROWS, 1), jnp.float32, math.log(0.4), math.log(3.0))) * ramp[:, None]
    col_scale = jnp.exp(jax.random.uniform(jax.random.fold_in(key, 4), (1, W), jnp.float32, math.log(0.6), math.log(1.6)))
    values = noise * row_scale * col_scale
    return values.astype(jnp.bfloat16)


def set_ends(result, rng, smallest, largest):
    longest = result.shape.index(max(result.shape))
    spots = []
    for shift in (0, 1):
        where = [jax.random.randint(jax.random.fold_in(rng, axis), (), 0, length) for axis, length in enumerate(result.shape)]
        where[longest] = (where[longest] + shift) % result.shape[longest]
        spots.append(tuple(where))
    return result.at[spots[0]].set(smallest).at[spots[1]].set(largest)


def shared_out(own_key, own, number, rows, count, top, reach, skew):
    order = jax.random.permutation(own_key, count)
    packed, common = load_shares(count, rows * top, reach, skew, True), load_shares(count, rows * top, reach, skew, False)
    places = jnp.arange(count)

    def named(tallies, turn):
        used = int((tallies > 0).sum())
        fixed = max(1, used // 4)
        shifted = fixed + (places - fixed + turn * (used - fixed)) % max(1, count - fixed)
        return jnp.zeros((count,), jnp.int32).at[order[jnp.where(places < fixed, places, shifted)]].set(jnp.asarray(tallies, jnp.int32))

    tallies = jnp.where(number % 4 == 0, named(packed, number // 4), named(common, number - number // 4 - 1))
    mixed = jax.random.permutation(jax.random.fold_in(own, 3), count)
    donor, sink = mixed[0:count // 2 * 2:2], mixed[1:count // 2 * 2:2]
    slack = jnp.minimum(tallies[donor] - 1, reach - tallies[sink]) // 2
    slack = jnp.where((donor == order[0]) | (sink == order[0]) | (tallies[sink] == 0), 0, jnp.maximum(slack, 0))
    shifted = jax.random.randint(jax.random.fold_in(own, 4), (count // 2,), 0, 1 << 20) % (slack + 1)
    tallies = tallies.at[donor].add(-shifted).at[sink].add(shifted)
    members = jnp.searchsorted(jnp.cumsum(tallies), jnp.arange(rows * top), side="right").astype(jnp.int32)
    grid = members.reshape(top, rows).T
    grid = grid[jax.random.permutation(jax.random.fold_in(own, 1), rows)]
    turn = jax.random.randint(jax.random.fold_in(own, 2), (rows, 1), 0, top)
    return jnp.take_along_axis(grid, (jnp.arange(top)[None, :] + turn) % top, axis=1)


def load_shares(amount, total, reach, skew, full):
    portions = [(1 << 20) // math.isqrt(standing ** skew) + 1 for standing in range(1, amount + 1)]
    largest = reach if full else min(reach, max(-(-total // amount), total * portions[0] // sum(portions)))
    least = 1 if total - largest >= amount - 1 else 0
    given, surplus = [largest] + [least] * (amount - 1), total - largest - least * (amount - 1)
    while surplus > 0:
        movable = [i for i in range(1, amount) if given[i] < largest] or [i for i in range(1, amount) if given[i] < reach]
        pool, left = sum([portions[i] for i in movable]), surplus
        for i in movable:
            more = min(reach - given[i], max(1, left * portions[i] // pool), surplus)
            given[i] = given[i] + more
            surplus = surplus - more
    return np.array(given)


def setup_inputs(seed: int = 0) -> dict:
    keys = jax.random.split(jax.random.key(seed), 5)
    queries = draw_queries(jax.random.fold_in(keys[4], 71), 0)
    slab = draw_slab(jax.random.fold_in(keys[4], 71), 0)
    cand_owner_keys = jax.random.split(jax.random.fold_in(keys[2], 1), Q // QD)
    cand_owner_turns = jax.random.permutation(jax.random.fold_in(keys[2], 3), Q // QD)
    cand_owner = jax.vmap(lambda own, number: shared_out(jax.random.fold_in(keys[2], 2), own, number, QD, DEVICES, K, CAP, 2))(cand_owner_keys, cand_owner_turns).reshape((Q, K))
    cand_row = set_ends(jax.random.randint(keys[3], (Q, K), 0, R_DEV), jax.random.fold_in(keys[3], 1), 0, R_DEV - 1).astype(jnp.int32)
    return {"queries": queries, "slab": slab, "cand_owner": cand_owner, "cand_row": cand_row}


def reference(queries, slab, cand_owner, cand_row):
    prefix_keys = slab[:, :PREFIX]
    blk = min(Q, 256)
    nblk = Q // blk
    scale = PREFIX ** -0.5

    def coarse(query_block):
        logits = lax.dot_general(query_block, prefix_keys, (((1,), (1,)), ((), ())), preferred_element_type=jnp.float32) * scale
        top = jnp.max(logits, axis=1)
        weights = jnp.exp(logits - top[:, None])
        total = jnp.sum(weights, axis=1)
        pooled_sum = jnp.dot(weights.astype(jnp.bfloat16), prefix_keys, preferred_element_type=jnp.float32)
        return pooled_sum / total[:, None], top + jnp.log(total)

    pooled, lse = lax.map(coarse, queries[:, :PREFIX].reshape(nblk, blk, PREFIX))
    pooled = pooled.reshape(Q, PREFIX)
    lse = lse.reshape(Q)
    cand = (cand_owner * R_DEV + cand_row).astype(jnp.int32)

    def fine(pair):
        query_block, id_block = pair
        rows = slab[id_block]
        return jnp.einsum("qw,qkw->qk", query_block.astype(jnp.float32), rows.astype(jnp.float32))

    full = lax.map(fine, (queries.reshape(nblk, blk, W), cand.reshape(nblk, blk, K)))
    full = full.reshape(Q, K) * (W ** -0.5)
    margin = full - lse[:, None]
    return pooled, lse, margin
```

```python
import functools
import math

import jax
import jax.numpy as jnp
from jax import lax
from jax.experimental import pallas as pl
from jax.experimental.pallas import tpu as pltpu
from jax.sharding import PartitionSpec as P

PREFIX = 256
LANES = 128
QB = 8
SLOTS = 4
F32 = jnp.float32
BF16 = jnp.bfloat16
ORDERS = ((1, 0, 2), (0, 2, 1), (2, 1, 0))
NT = (((1,), (1,)), ((), ()))
M_LANE = 127
L_LANE = 96
F_LANE = 64


def lane_of(rows):
    return lax.broadcasted_iota(jnp.int32, (rows, LANES), 1)


def merge(part, blocks):
    lane = lane_of(blocks[0].shape[0])
    maxima = [b[:, M_LANE:] for b in blocks]
    top = functools.reduce(jnp.maximum, maxima)
    total = None
    for b, m in zip(blocks, maxima):
        s = jnp.broadcast_to(jnp.exp2(m - top), b.shape)
        if part == 2:
            s = jnp.where((lane >= F_LANE) & (lane < L_LANE), 1.0, s)
        total = b * s if total is None else total + b * s
    return jnp.where(lane == M_LANE, top, total)


def kernel(
    dims,
    col0,
    q_ref,
    slab_ref,
    own_ref,
    row_ref,
    pooled_ref,
    lse_ref,
    margin_ref,
    slab_v,
    x_buf,
    f0,
    f1,
    f2,
    sel_buf,
    hot,
    rows_buf,
    logits,
    pay,
    got0,
    mid0,
    got1,
    mid1,
    got2,
    mid2,
    got3,
    lsem,
    xs,
    xr,
    fs,
    fr,
    rs,
    rr,
):
    width = q_ref.shape[1]
    r_dev = slab_ref.shape[0]
    ii, qq = lax.axis_index("index"), lax.axis_index("query")
    coord = (lax.div(ii, dims[1]), lax.rem(ii, dims[1]), lax.div(qq, 2))
    core = lax.rem(qq, 2)
    me = ii * (dims[2] * 2) + qq
    chunk = dims[1] * dims[2] * 2 * QB
    k_count = row_ref.shape[1]
    f_bufs = (f0, f1, f2)

    def device(at, c):
        return (at[0] * dims[1] + at[1], at[2] * 2 + c)

    def peer(axis, k):
        at = list(coord)
        at[axis] = lax.rem(coord[axis] + k, dims[axis])
        return tuple(at)

    sibling = device(coord, 1 - core)

    pre_copy = pltpu.make_async_copy(
        slab_ref.at[:, pl.ds(0, PREFIX)], slab_v.at[:, pl.ds(0, PREFIX)], lsem.at[0]
    )
    rest_copy = pltpu.make_async_copy(
        slab_ref.at[:, pl.ds(PREFIX, width - PREFIX)],
        slab_v.at[:, pl.ds(PREFIX, width - PREFIX)],
        lsem.at[1],
    )
    pre_copy.start()
    rest_copy.start()

    barrier = pltpu.get_barrier_semaphore()
    n_peers = 1
    pl.semaphore_signal(barrier, inc=1, device_id=sibling, device_id_type=pl.DeviceIdType.MESH)
    for axis in range(3):
        for k in range(1, dims[axis]):
            n_peers += 1
            pl.semaphore_signal(
                barrier, inc=1, device_id=device(peer(axis, k), core), device_id_type=pl.DeviceIdType.MESH
            )

    here = coord + (core,)
    x_buf[(0,) + here] = q_ref[:, 0:LANES]
    x_buf[(1,) + here] = q_ref[:, LANES:PREFIX]
    row = row_ref[...]
    numbers = jnp.concatenate(
        [
            own_ref[...].astype(F32),
            lax.shift_right_logical(row, 6).astype(F32),
            (row & 63).astype(F32),
            jnp.zeros((QB, LANES - 3 * row.shape[1]), F32),
        ],
        axis=1,
    )
    x_buf[(2,) + here] = numbers.astype(BF16)
    for p in range(3):
        f_bufs[p][here] = q_ref[:, col0[p] : col0[p + 1]]
    pl.semaphore_wait(barrier, n_peers)

    def copy(src, dst, ssem, rsem, target):
        return pltpu.make_async_remote_copy(
            src_ref=src,
            dst_ref=dst,
            send_sem=ssem,
            recv_sem=rsem,
            device_id=target,
            device_id_type=pl.DeviceIdType.MESH,
        )

    def gather_step(bufs, ssem, rsem, phase):
        started = []
        for p in range(3):
            if phase == 3:
                block = bufs[p].at[:, :, :, core]
                targets = [sibling]
            else:
                done = ORDERS[p][:phase]
                where = tuple(slice(None) if a in done else coord[a] for a in range(3))
                block = bufs[p].at[where + (core,)]
                axis = ORDERS[p][phase]
                targets = [device(peer(axis, k), core) for k in range(1, dims[axis])]
            for k, target in enumerate(targets):
                at = (p * 4 + phase) * 3 + k
                c = copy(block, block, ssem.at[at], rsem.at[at], target)
                c.start()
                started.append(c)
        return started

    x_bufs = [x_buf.at[p] for p in range(3)]
    sent = []

    def arrived(copies):
        for c in copies:
            c.wait_recv()
        sent.extend(copies)

    x_now = gather_step(x_bufs, xs, xr, 0)
    f_now = gather_step(f_bufs, fs, fr, 0)
    arrived(x_now)
    x_now = gather_step(x_bufs, xs, xr, 1)
    arrived(f_now)
    arrived(x_now)
    x_now = gather_step(x_bufs, xs, xr, 2)
    f_now = gather_step(f_bufs, fs, fr, 1)
    arrived(x_now)
    x_now = gather_step(x_bufs, xs, xr, 3)
    arrived(f_now)
    f_now = gather_step(f_bufs, fs, fr, 2)
    arrived(x_now)

    def x_part(p, y):
        return x_buf[p, y].astype(F32).reshape(chunk, LANES)

    me_f = me.astype(F32)
    n_slot = chunk // QB * SLOTS

    @pl.loop(0, dims[0])
    def _(y):
        numbers = x_part(2, y)
        lane = lane_of(chunk)
        hit = (numbers == me_f) & (lane < k_count)
        high = pltpu.roll(numbers, LANES - k_count, 1)
        low = pltpu.roll(numbers, LANES - 2 * k_count, 1)
        any_hit = jnp.sum(jnp.where(hit, 1.0, 0.0), axis=1, keepdims=True)
        high = jnp.sum(jnp.where(hit, high, 0.0), axis=1, keepdims=True)
        low = jnp.sum(jnp.where(hit, low, 0.0), axis=1, keepdims=True)
        qi = lax.broadcasted_iota(jnp.int32, (chunk, chunk), 0)
        qj = lax.broadcasted_iota(jnp.int32, (chunk, chunk), 1)
        before = jnp.where(((qi >> 3) == (qj >> 3)) & (qj < qi), 1.0, 0.0).astype(BF16)
        rank = jnp.dot(
            before,
            jnp.broadcast_to(any_hit, (chunk, LANES)).astype(BF16),
            preferred_element_type=F32,
        )[:, 0:1]
        rank = jnp.where(any_hit > 0.0, rank, -1.0)
        q_of = lax.broadcasted_iota(jnp.int32, (chunk, n_slot), 0)
        s_of = lax.broadcasted_iota(jnp.int32, (chunk, n_slot), 1)
        sel = jnp.where(
            ((q_of >> 3) == (s_of >> 2)) & (rank == (s_of & 3).astype(F32)), 1.0, 0.0
        )
        sel_buf[y] = sel
        picked = jnp.dot(
            sel.T.astype(BF16),
            jnp.where(lane < 64, high, low).astype(BF16),
            preferred_element_type=F32,
        )
        row_of = (picked[:, 0:1] * 64.0 + picked[:, 64:65]).astype(jnp.int32)
        rows = pl.ds(pl.multiple_of(y * n_slot, n_slot), n_slot)
        for t in range(r_dev // 512):
            r = lax.broadcasted_iota(jnp.int32, (n_slot, 512), 1) + t * 512
            hot[rows, t * 512 : (t + 1) * 512] = jnp.where(r == row_of, 1.0, 0.0).astype(BF16)

    pre_copy.wait()
    rest_copy.wait()

    @pl.loop(0, width // 256)
    def _(n):
        cols = pl.ds(pl.multiple_of(n * 256, 256), 256)
        rows_buf[:, cols] = jnp.dot(hot[...], slab_v[:, cols], preferred_element_type=F32).astype(BF16)

    arrived(f_now)
    f_now = gather_step(f_bufs, fs, fr, 3)

    factor = PREFIX ** (-0.5) * math.log2(math.e)
    tile = 512

    @pl.loop(0, dims[0])
    def _(y):
        q = jnp.concatenate([x_part(0, y), x_part(1, y)], axis=1).astype(BF16)
        most = jnp.full((chunk, LANES), -jnp.inf, F32)
        for t in range(r_dev // tile):
            s = lax.dot_general(
                q, slab_v[t * tile : (t + 1) * tile, 0:PREFIX], NT, preferred_element_type=F32
            )
            logits[:, t * tile : (t + 1) * tile] = s
            for u in range(tile // LANES):
                most = jnp.maximum(most, s[:, u * LANES : (u + 1) * LANES])
        top = jnp.max(most, axis=1, keepdims=True) * factor
        total = jnp.zeros((chunk, LANES), F32)
        acc = jnp.zeros((chunk, PREFIX), F32)
        for t in range(r_dev // tile):
            w = jnp.exp2(logits[:, t * tile : (t + 1) * tile] * factor - top)
            for u in range(tile // LANES):
                total = total + w[:, u * LANES : (u + 1) * LANES]
            acc = acc + jnp.dot(
                w.astype(BF16), slab_v[t * tile : (t + 1) * tile, 0:PREFIX], preferred_element_type=F32
            )
        total = jnp.sum(total, axis=1, keepdims=True)
        lane = lane_of(chunk)
        p0, p1 = acc[:, :LANES], acc[:, LANES:]
        r1 = pltpu.roll(p1, 32, 1)
        shape = (dims[1], dims[2], 2, QB, LANES)
        pay[0, y] = jnp.where(lane == M_LANE, top, p0).reshape(shape)
        b = jnp.where(lane < 32, pltpu.roll(p0, 32, 1), r1)
        pay[1, y] = jnp.where(lane == M_LANE, top, b).reshape(shape)
        c = jnp.where(lane < F_LANE, pltpu.roll(p1, 64, 1), 0.0)
        c = jnp.where(lane == L_LANE, total, c)
        pay[2, y] = jnp.where(lane == M_LANE, top, c).reshape(shape)

    arrived(f_now)

    @pl.loop(0, dims[0])
    def _(y):
        rows = pl.ds(pl.multiple_of(y * n_slot, n_slot), n_slot)
        q = jnp.concatenate([x_part(0, y), x_part(1, y)], axis=1).astype(BF16)
        scores = lax.dot_general(q, rows_buf[rows, 0:PREFIX], NT, preferred_element_type=F32)
        for p in range(3):
            q = f_bufs[p][y].astype(F32).reshape(chunk, col0[p + 1] - col0[p]).astype(BF16)
            scores = scores + lax.dot_general(
                q, rows_buf[rows, col0[p] : col0[p + 1]], NT, preferred_element_type=F32
            )
        full = jnp.sum(scores * sel_buf[y], axis=1, keepdims=True)
        lane = lane_of(chunk)
        mine = jnp.where((x_part(2, y) == me_f) & (lane < k_count), full, 0.0)
        mine = pltpu.roll(mine, F_LANE, 1)
        pay[2, y] = pay[2, y] + mine.reshape(dims[1], dims[2], 2, QB, LANES)

    def at_part(p):
        return p * 4 * 3

    now = []
    for p in range(3):
        at = at_part(p)
        c = copy(pay.at[p, :, :, :, 1 - core], got0.at[p], rs.at[at], rr.at[at], sibling)
        c.start()
        now.append(c)
    flat0 = (dims[0] * dims[1] * dims[2] * QB, LANES)
    for p in range(3):
        now[p].wait_recv()
        a = pay[p, :, :, :, core].reshape(flat0)
        mid0[p] = merge(p, [a, got0[p].reshape(flat0)]).reshape(dims + (QB, LANES))
        sent.append(now[p])

        axis = ORDERS[p][0]
        started = []
        for k in range(1, dims[axis]):
            where = tuple(peer(axis, k)[a] if a == axis else slice(None) for a in range(3))
            at = at_part(p) + 3 + k - 1
            c = copy(mid0.at[(p,) + where], got1.at[p, k - 1], rs.at[at], rr.at[at], device(peer(axis, k), core))
            c.start()
            started.append(c)
        now[p] = started

    def pick(value_ref, axis, index):
        where = tuple(index if a == axis else slice(None) for a in range(3))
        return where

    for p in range(3):
        arrived(now[p])
        first, second, third = ORDERS[p]
        n1 = [dims[a] for a in range(3) if a != first]
        flat1 = (n1[0] * n1[1] * QB, LANES)
        own = mid0[(p,) + pick(mid0, first, coord[first])].reshape(flat1)
        blocks = [own] + [got1[p, k - 1].reshape(flat1) for k in range(1, dims[first])]
        mid1[p] = merge(p, blocks).reshape(n1[0], n1[1], QB, LANES)
        left = [a for a in range(3) if a != first]
        started = []
        for k in range(1, dims[second]):
            to = peer(second, k)
            where = tuple(to[a] if a == second else slice(None) for a in left)
            at = at_part(p) + 6 + k - 1
            c = copy(mid1.at[(p,) + where], got2.at[p, k - 1], rs.at[at], rr.at[at], device(to, core))
            c.start()
            started.append(c)
        now[p] = started

    for p in range(3):
        arrived(now[p])
        first, second, third = ORDERS[p]
        left = [a for a in range(3) if a != first]
        flat2 = (dims[third] * QB, LANES)
        where = tuple(coord[a] if a == second else slice(None) for a in left)
        own = mid1[(p,) + where].reshape(flat2)
        blocks = [own] + [got2[p, k - 1].reshape(flat2) for k in range(1, dims[second])]
        mid2[p] = merge(p, blocks).reshape(dims[third], QB, LANES)
        started = []
        for k in range(1, dims[third]):
            to = peer(third, k)
            at = at_part(p) + 9 + k - 1
            c = copy(mid2.at[p, to[third]], got3.at[p, k - 1], rs.at[at], rr.at[at], device(to, core))
            c.start()
            started.append(c)
        now[p] = started

    out = []
    for p in range(3):
        arrived(now[p])
        third = ORDERS[p][2]
        own = mid2[p, coord[third]]
        out.append(merge(p, [own] + [got3[p, k - 1] for k in range(1, dims[third])]))

    lane = lane_of(QB)
    a, b, c = out
    total = c[:, L_LANE : L_LANE + 1]
    top = c[:, M_LANE:]
    b_back = pltpu.roll(b, 96, 1)
    pooled_ref[:, 0:LANES] = jnp.where(lane < 96, a, b_back) / total
    pooled_ref[:, LANES:PREFIX] = jnp.where(lane < 64, b_back, pltpu.roll(c, 64, 1)) / total
    lse = top * math.log(2.0) + jnp.log(total)
    lse_ref[...] = lse
    full = pltpu.roll(c, LANES - F_LANE, 1) * width ** (-0.5)
    margin_ref[...] = (full - lse)[:, : margin_ref.shape[1]]

    for c in sent:
        c.wait_send()


def make(mesh, dims):
    def on_device(queries, slab, cand_owner, cand_row):
        width = queries.shape[1]
        r_dev = slab.shape[0]
        k_count = cand_owner.shape[1]
        tiles = (width - PREFIX) // LANES
        n0 = -(-tiles // 3)
        n1 = -(-(tiles - n0) // 2)
        col0 = (PREFIX, PREFIX + n0 * LANES, PREFIX + (n0 + n1) * LANES, width)
        n_chunk = dims[1] * dims[2] * 2 * QB
        n_slot = n_chunk // QB * SLOTS
        side = max(dims)
        vmem = pltpu.VMEM
        dma = pltpu.SemaphoreType.DMA
        spec = pl.BlockSpec(memory_space=pltpu.VMEM)
        pooled, lse, margin = pl.pallas_call(
            functools.partial(kernel, dims, col0),
            out_shape=(
                jax.ShapeDtypeStruct((QB, PREFIX), F32),
                jax.ShapeDtypeStruct((QB, 1), F32),
                jax.ShapeDtypeStruct((QB, k_count), F32),
            ),
            in_specs=[spec, pl.BlockSpec(memory_space=pl.ANY), spec, spec],
            out_specs=(spec, spec, spec),
            scratch_shapes=[
                vmem((r_dev, width), BF16),
                vmem((3,) + dims + (2, QB, LANES), BF16),
                vmem(dims + (2, QB, col0[1] - col0[0]), BF16),
                vmem(dims + (2, QB, col0[2] - col0[1]), BF16),
                vmem(dims + (2, QB, col0[3] - col0[2]), BF16),
                vmem((dims[0], n_chunk, n_slot), F32),
                vmem((dims[0] * n_slot, r_dev), BF16),
                vmem((dims[0] * n_slot, width), BF16),
                vmem((n_chunk, r_dev), F32),
                vmem((3,) + dims + (2, QB, LANES), F32),
                vmem((3,) + dims + (QB, LANES), F32),
                vmem((3,) + dims + (QB, LANES), F32),
                vmem((3, side - 1, side, side, QB, LANES), F32),
                vmem((3, side, side, QB, LANES), F32),
                vmem((3, side - 1, side, QB, LANES), F32),
                vmem((3, side, QB, LANES), F32),
                vmem((3, side - 1, QB, LANES), F32),
                dma((2,)),
                dma((36,)),
                dma((36,)),
                dma((36,)),
                dma((36,)),
                dma((36,)),
                dma((36,)),
            ],
            compiler_params=pltpu.CompilerParams(
                collective_id=0, has_side_effects=True, vmem_limit_bytes=56 * 2**20
            ),
        )(queries, slab, cand_owner, cand_row)
        return pooled, lse.reshape(QB), margin

    both = ("index", "query")
    return jax.shard_map(
        on_device,
        mesh=mesh,
        in_specs=(P(both, None),) * 4,
        out_specs=(P(both, None), P(both), P(both, None)),
        check_vma=False,
    )


def solution(mesh):
    side = math.isqrt(mesh.shape["index"])
    return make(mesh, (side, side, mesh.shape["query"] // 2))
```

```python
import functools
import math

import jax
import jax.numpy as jnp
from jax import lax
from jax.experimental import pallas as pl
from jax.experimental.pallas import tpu as pltpu
from jax.sharding import PartitionSpec as P

PREFIX = 256
LANES = 128
QB = 8
SLOTS = 4
F32 = jnp.float32
BF16 = jnp.bfloat16
ORDERS = ((1, 0, 2), (0, 2, 1), (2, 1, 0))
NT = (((1,), (1,)), ((), ()))
M_LANE = 127
L_LANE = 96
F_LANE = 64


def lane_of(rows):
    return lax.broadcasted_iota(jnp.int32, (rows, LANES), 1)


def merge(part, blocks):
    lane = lane_of(blocks[0].shape[0])
    maxima = [b[:, M_LANE:] for b in blocks]
    top = functools.reduce(jnp.maximum, maxima)
    total = None
    for b, m in zip(blocks, maxima):
        s = jnp.broadcast_to(jnp.exp2(m - top), b.shape)
        if part == 2:
            s = jnp.where((lane >= F_LANE) & (lane < L_LANE), 1.0, s)
        total = b * s if total is None else total + b * s
    return jnp.where(lane == M_LANE, top, total)


def kernel(
    dims,
    col0,
    q_ref,
    slab_ref,
    own_ref,
    row_ref,
    out_ref,
    slab_v,
    x_buf,
    f0,
    f1,
    f2,
    sel_buf,
    hot,
    rows_buf,
    logits,
    pay,
    got0,
    mid0,
    got1,
    mid1,
    got2,
    mid2,
    got3,
    lsem,
    xs,
    xr,
    fs,
    fr,
    s0,
    r0,
    rs,
    rr,
):
    width = q_ref.shape[1]
    r_dev = slab_ref.shape[0]
    ii, qq = lax.axis_index("index"), lax.axis_index("query")
    coord = (lax.div(ii, dims[1]), lax.rem(ii, dims[1]), lax.div(qq, 2))
    core = lax.rem(qq, 2)
    me_f = (ii * (dims[2] * 2) + qq).astype(F32)
    n = dims[0]
    pairs = n // 2
    k_count = row_ref.shape[1]
    box = (2, n, n, QB, LANES)
    chunk = 2 * n * n * QB
    n_slot = chunk // QB * SLOTS
    f_bufs = (f0, f1, f2)
    x_bufs = [x_buf.at[p] for p in range(3)]

    def device(at, c):
        return (at[0] * n + at[1], at[2] * 2 + c)

    def peer(axis, k):
        at = list(coord)
        at[axis] = lax.rem(coord[axis] + k, n)
        return tuple(at)

    sibling = device(coord, 1 - core)

    pre_copy = pltpu.make_async_copy(
        slab_ref.at[:, pl.ds(0, PREFIX)], slab_v.at[:, pl.ds(0, PREFIX)], lsem.at[0]
    )
    rest_copy = pltpu.make_async_copy(
        slab_ref.at[:, pl.ds(PREFIX, width - PREFIX)],
        slab_v.at[:, pl.ds(PREFIX, width - PREFIX)],
        lsem.at[1],
    )

    barrier = pltpu.get_barrier_semaphore()
    pl.semaphore_signal(barrier, inc=1, device_id=sibling, device_id_type=pl.DeviceIdType.MESH)
    for axis in range(3):
        for k in range(1, n):
            pl.semaphore_signal(
                barrier, inc=1, device_id=device(peer(axis, k), core), device_id_type=pl.DeviceIdType.MESH
            )
    pre_copy.start()
    rest_copy.start()

    here = coord + (core,)
    x_buf[(0,) + here] = q_ref[:, 0:LANES]
    x_buf[(1,) + here] = q_ref[:, LANES:PREFIX]
    row = row_ref[...]
    numbers = jnp.concatenate(
        [
            own_ref[...].astype(F32),
            lax.shift_right_logical(row, 6).astype(F32),
            (row & 63).astype(F32),
            jnp.zeros((QB, LANES - 3 * k_count), F32),
        ],
        axis=1,
    )
    x_buf[(2,) + here] = numbers.astype(BF16)
    for p in range(3):
        f_bufs[p][here] = q_ref[:, col0[p] : col0[p + 1]]
    pl.semaphore_wait(barrier, 1 + 3 * (n - 1))

    def send(src, dst, ssem, rsem, target):
        pltpu.make_async_remote_copy(
            src_ref=src,
            dst_ref=dst,
            send_sem=ssem,
            recv_sem=rsem,
            device_id=target,
            device_id_type=pl.DeviceIdType.MESH,
        ).start()

    def wait_bytes(ref, sem):
        pltpu.make_async_copy(ref, ref, sem).wait()

    def phase_box(phase):
        if phase == 3:
            return (slice(None),) * 3 + (0,)
        return (slice(0, n - 1),) + (slice(None),) * phase + (0,) * (2 - phase) + (0,)

    def gather_start(bufs, ssem_of, rsem, phase, p):
        if phase == 3:
            block = bufs[p].at[:, :, :, core]
            targets = [sibling]
        else:
            done = ORDERS[p][:phase]
            where = tuple(slice(None) if a in done else coord[a] for a in range(3))
            block = bufs[p].at[where + (core,)]
            axis = ORDERS[p][phase]
            targets = [device(peer(axis, k), core) for k in range(1, n)]
        for target in targets:
            send(block, block, ssem_of(p, phase), rsem.at[p * 4 + phase], target)

    def x_ssem(p, phase):
        return xs.at[phase]

    def f_ssem(p, phase):
        return fs.at[p * 4 + phase]

    def x_start(phase):
        for p in range(3):
            gather_start(x_bufs, x_ssem, xr, phase, p)

    def f_start(phase):
        for p in range(3):
            gather_start(f_bufs, f_ssem, fr, phase, p)

    def x_step(phase):
        for p in range(3):
            wait_bytes(x_bufs[p].at[phase_box(phase)], xr.at[p * 4 + phase])
            if phase < 3:
                gather_start(x_bufs, x_ssem, xr, phase + 1, p)

    def f_step(phase):
        for p in range(3):
            wait_bytes(f_bufs[p].at[phase_box(phase)], fr.at[p * 4 + phase])
            if phase < 3:
                gather_start(f_bufs, f_ssem, fr, phase + 1, p)

    x_start(0)
    f_start(0)
    x_step(0)
    x_step(1)
    f_step(0)
    x_step(2)
    f_step(1)

    def part_of(buf, t, c):
        v = buf[pl.ds(2 * t, 2), :, :, c]
        return v.astype(F32).reshape(chunk, v.shape[-1])

    def index(j, t, c):
        numbers = part_of(x_bufs[2], t, c)
        lane = lane_of(chunk)
        hit = (numbers == me_f) & (lane < k_count)
        high = pltpu.roll(numbers, LANES - k_count, 1)
        low = pltpu.roll(numbers, LANES - 2 * k_count, 1)
        any_hit = jnp.sum(jnp.where(hit, 1.0, 0.0), axis=1, keepdims=True)
        high = jnp.sum(jnp.where(hit, high, 0.0), axis=1, keepdims=True)
        low = jnp.sum(jnp.where(hit, low, 0.0), axis=1, keepdims=True)
        qi = lax.broadcasted_iota(jnp.int32, (chunk, chunk), 0)
        qj = lax.broadcasted_iota(jnp.int32, (chunk, chunk), 1)
        before = jnp.where(((qi >> 3) == (qj >> 3)) & (qj < qi), 1.0, 0.0).astype(BF16)
        rank = jnp.dot(
            before,
            jnp.broadcast_to(any_hit, (chunk, LANES)).astype(BF16),
            preferred_element_type=F32,
        )[:, 0:1]
        rank = jnp.where(any_hit > 0.0, rank, -1.0)
        q_of = lax.broadcasted_iota(jnp.int32, (chunk, n_slot), 0)
        s_of = lax.broadcasted_iota(jnp.int32, (chunk, n_slot), 1)
        sel = jnp.where(
            ((q_of >> 3) == (s_of >> 2)) & (rank == (s_of & 3).astype(F32)), 1.0, 0.0
        )
        sel_buf[j] = sel
        picked = jnp.dot(
            sel.T.astype(BF16),
            jnp.where(lane < 64, high, low).astype(BF16),
            preferred_element_type=F32,
        )
        row_of = (picked[:, 0:1] * 64.0 + picked[:, 64:65]).astype(jnp.int32)
        rows = pl.ds(pl.multiple_of(j * n_slot, n_slot), n_slot)
        for u in range(r_dev // 512):
            r = lax.broadcasted_iota(jnp.int32, (n_slot, 512), 1) + u * 512
            hot[rows, u * 512 : (u + 1) * 512] = jnp.where(r == row_of, 1.0, 0.0).astype(BF16)

    @pl.loop(0, pairs)
    def _(t):
        index(t, t, core)

    x_step(3)

    @pl.loop(0, pairs)
    def _(t):
        index(pairs + t, t, 1 - core)

    pre_copy.wait()
    rest_copy.wait()

    def pick_rows(i):
        cols = pl.ds(pl.multiple_of(i * 256, 256), 256)
        rows_buf[:, cols] = jnp.dot(hot[...], slab_v[:, cols], preferred_element_type=F32).astype(BF16)

    half = width // 512

    @pl.loop(0, half)
    def _(i):
        pick_rows(i)

    f_step(2)

    @pl.loop(half, width // 256)
    def _(i):
        pick_rows(i)

    f_step(3)

    factor = PREFIX ** (-0.5) * math.log2(math.e)
    tile = 512

    def score(j, t, c):
        q = jnp.concatenate([part_of(x_bufs[0], t, c), part_of(x_bufs[1], t, c)], axis=1).astype(BF16)
        most = jnp.full((chunk, LANES), -jnp.inf, F32)
        for u in range(r_dev // tile):
            s = lax.dot_general(
                q, slab_v[u * tile : (u + 1) * tile, 0:PREFIX], NT, preferred_element_type=F32
            )
            logits[:, u * tile : (u + 1) * tile] = s
            for v in range(tile // LANES):
                most = jnp.maximum(most, s[:, v * LANES : (v + 1) * LANES])
        top = jnp.max(most, axis=1, keepdims=True) * factor
        total = jnp.zeros((chunk, LANES), F32)
        acc = jnp.zeros((chunk, PREFIX), F32)
        for u in range(r_dev // tile):
            w = jnp.exp2(logits[:, u * tile : (u + 1) * tile] * factor - top)
            for v in range(tile // LANES):
                total = total + w[:, v * LANES : (v + 1) * LANES]
            acc = acc + jnp.dot(
                w.astype(BF16), slab_v[u * tile : (u + 1) * tile, 0:PREFIX], preferred_element_type=F32
            )
        total = jnp.sum(total, axis=1, keepdims=True)

        rows = pl.ds(pl.multiple_of(j * n_slot, n_slot), n_slot)
        scores = lax.dot_general(q, rows_buf[rows, 0:PREFIX], NT, preferred_element_type=F32)
        for p in range(3):
            scores = scores + lax.dot_general(
                part_of(f_bufs[p], t, c).astype(BF16),
                rows_buf[rows, col0[p] : col0[p + 1]],
                NT,
                preferred_element_type=F32,
            )
        full = jnp.sum(scores * sel_buf[j], axis=1, keepdims=True)

        lane = lane_of(chunk)
        full = jnp.where((part_of(x_bufs[2], t, c) == me_f) & (lane < k_count), full, 0.0)
        p0, p1 = acc[:, :LANES], acc[:, LANES:]
        b = jnp.where(lane < 32, pltpu.roll(p0, 32, 1), pltpu.roll(p1, 32, 1))
        c = jnp.where(lane < F_LANE, pltpu.roll(p1, 64, 1), pltpu.roll(full, F_LANE, 1))
        c = jnp.where(lane == L_LANE, total, c)
        return [jnp.where(lane == M_LANE, top, v) for v in (p0, b, c)]

    @pl.loop(0, pairs)
    def _(t):
        for p, v in enumerate(score(pairs + t, t, 1 - core)):
            pay[t, p] = v.reshape(box)
        send(pay.at[t], got0.at[t], s0.at[t], r0.at[t], sibling)

    @pl.loop(0, pairs)
    def _(t):
        mine = score(t, t, core)
        wait_bytes(got0.at[t], r0.at[t])
        for p in range(3):
            both = merge(p, [mine[p], got0[t, p].reshape(chunk, LANES)])
            mid0[p, pl.ds(2 * t, 2)] = both.reshape(box)

    def at_axis(axes, axis, index):
        return tuple(index if a == axis else slice(None) for a in axes)

    for p in range(3):
        axis = ORDERS[p][0]
        for k in range(1, n):
            to = peer(axis, k)
            send(mid0.at[(p,) + at_axis(range(3), axis, to[axis])], got1.at[p, k - 1], rs.at[0], rr.at[p], device(to, core))

    flat1 = (n * n * QB, LANES)
    for p in range(3):
        wait_bytes(got1.at[p], rr.at[p])
        first, second, third = ORDERS[p]
        own = mid0[(p,) + at_axis(range(3), first, coord[first])].reshape(flat1)
        blocks = [own] + [got1[p, k - 1].reshape(flat1) for k in range(1, n)]
        mid1[p] = merge(p, blocks).reshape(n, n, QB, LANES)
        left = [a for a in range(3) if a != first]
        for k in range(1, n):
            to = peer(second, k)
            send(mid1.at[(p,) + at_axis(left, second, to[second])], got2.at[p, k - 1], rs.at[1], rr.at[3 + p], device(to, core))

    flat2 = (n * QB, LANES)
    for p in range(3):
        wait_bytes(got2.at[p], rr.at[3 + p])
        first, second, third = ORDERS[p]
        left = [a for a in range(3) if a != first]
        own = mid1[(p,) + at_axis(left, second, coord[second])].reshape(flat2)
        blocks = [own] + [got2[p, k - 1].reshape(flat2) for k in range(1, n)]
        mid2[p] = merge(p, blocks).reshape(n, QB, LANES)
        for k in range(1, n):
            to = peer(third, k)
            send(mid2.at[p, to[third]], got3.at[p, k - 1], rs.at[2], rr.at[6 + p], device(to, core))

    out = []
    for p in range(3):
        wait_bytes(got3.at[p], rr.at[6 + p])
        own = mid2[p, coord[ORDERS[p][2]]]
        out.append(merge(p, [own] + [got3[p, k - 1] for k in range(1, n)]))

    lane = lane_of(QB)
    a, b, c = out
    total = c[:, L_LANE : L_LANE + 1]
    b_back = pltpu.roll(b, 96, 1)
    out_ref[:, 0:LANES] = jnp.where(lane < 96, a, b_back) / total
    out_ref[:, LANES:PREFIX] = jnp.where(lane < 64, b_back, pltpu.roll(c, 64, 1)) / total
    lse = c[:, M_LANE:] * math.log(2.0) + jnp.log(total)
    full = pltpu.roll(c, LANES - F_LANE, 1) * width ** (-0.5)
    out_ref[:, PREFIX : PREFIX + LANES] = full - lse
    out_ref[:, PREFIX + LANES :] = jnp.broadcast_to(lse, (QB, LANES))

    for phase in range(4):
        wait_bytes(x_buf.at[(slice(None),) + phase_box(phase)], xs.at[phase])
        for p in range(3):
            wait_bytes(f_bufs[p].at[phase_box(phase)], fs.at[p * 4 + phase])
    for t in range(pairs):
        wait_bytes(pay.at[t], s0.at[t])
    wait_bytes(got1, rs.at[0])
    wait_bytes(got2, rs.at[1])
    wait_bytes(got3, rs.at[2])


def split(in_ref, pooled_ref, lse_ref, margin_ref):
    pooled_ref[...] = in_ref[:, 0:PREFIX]
    margin_ref[...] = in_ref[:, PREFIX : PREFIX + margin_ref.shape[1]]
    here = lax.broadcasted_iota(jnp.int32, (QB, LANES), 0) == lane_of(QB)
    lse = jnp.sum(jnp.where(here, in_ref[:, PREFIX + LANES :], 0.0), axis=0, keepdims=True)
    lse_ref[...] = lse[:, 0:QB]


def make(mesh, dims):
    def on_device(queries, slab, cand_owner, cand_row):
        width = queries.shape[1]
        r_dev = slab.shape[0]
        k_count = cand_owner.shape[1]
        tiles = (width - PREFIX) // LANES
        n0 = -(-tiles // 3)
        n1 = -(-(tiles - n0) // 2)
        col0 = (PREFIX, PREFIX + n0 * LANES, PREFIX + (n0 + n1) * LANES, width)
        n = dims[0]
        chunk = 2 * n * n * QB
        n_slot = chunk // QB * SLOTS
        vmem = pltpu.VMEM
        dma = pltpu.SemaphoreType.DMA
        spec = pl.BlockSpec(memory_space=pltpu.VMEM)
        merged = pl.pallas_call(
            functools.partial(kernel, dims, col0),
            out_shape=jax.ShapeDtypeStruct((QB, PREFIX + 2 * LANES), F32),
            in_specs=[spec, pl.BlockSpec(memory_space=pl.ANY), spec, spec],
            out_specs=spec,
            scratch_shapes=[
                vmem((r_dev, width), BF16),
                vmem((3, n, n, n, 2, QB, LANES), BF16),
                vmem((n, n, n, 2, QB, col0[1] - col0[0]), BF16),
                vmem((n, n, n, 2, QB, col0[2] - col0[1]), BF16),
                vmem((n, n, n, 2, QB, col0[3] - col0[2]), BF16),
                vmem((n, chunk, n_slot), F32),
                vmem((n * n_slot, r_dev), BF16),
                vmem((n * n_slot, width), BF16),
                vmem((chunk, r_dev), F32),
                vmem((n // 2, 3, 2, n, n, QB, LANES), F32),
                vmem((n // 2, 3, 2, n, n, QB, LANES), F32),
                vmem((3, n, n, n, QB, LANES), F32),
                vmem((3, n - 1, n, n, QB, LANES), F32),
                vmem((3, n, n, QB, LANES), F32),
                vmem((3, n - 1, n, QB, LANES), F32),
                vmem((3, n, QB, LANES), F32),
                vmem((3, n - 1, QB, LANES), F32),
                dma((2,)),
                dma((4,)),
                dma((12,)),
                dma((12,)),
                dma((12,)),
                dma((n // 2,)),
                dma((n // 2,)),
                dma((3,)),
                dma((9,)),
            ],
            compiler_params=pltpu.CompilerParams(
                collective_id=0, has_side_effects=True, vmem_limit_bytes=56 * 2**20
            ),
        )(queries, slab, cand_owner, cand_row)
        pooled, lse, margin = pl.pallas_call(
            split,
            out_shape=(
                jax.ShapeDtypeStruct((QB, PREFIX), F32),
                jax.ShapeDtypeStruct((1, QB), F32),
                jax.ShapeDtypeStruct((QB, k_count), F32),
            ),
            in_specs=[spec],
            out_specs=(spec, spec, spec),
        )(merged)
        return pooled, lse.reshape(QB), margin

    both = ("index", "query")
    return jax.shard_map(
        on_device,
        mesh=mesh,
        in_specs=(P(both, None),) * 4,
        out_specs=(P(both, None), P(both), P(both, None)),
        check_vma=False,
    )


def solution(mesh):
    side = math.isqrt(mesh.shape["index"])
    return make(mesh, (side, side, mesh.shape["query"] // 2))
```

```python
import functools
import math

import jax
import jax.numpy as jnp
from jax import lax
from jax.experimental import pallas as pl
from jax.experimental.pallas import tpu as pltpu
from jax.sharding import PartitionSpec as P

PREFIX = 256
LANES = 128
QB = 8
SLOTS = 4
F32 = jnp.float32
BF16 = jnp.bfloat16
ORDERS = ((1, 0, 2), (0, 2, 1), (2, 1, 0))
NT = (((1,), (1,)), ((), ()))
M_LANE = 127
L_LANE = 96
F_LANE = 64


def lane_of(rows):
    return lax.broadcasted_iota(jnp.int32, (rows, LANES), 1)


def merge(part, blocks):
    lane = lane_of(blocks[0].shape[0])
    maxima = [b[:, M_LANE:] for b in blocks]
    top = functools.reduce(jnp.maximum, maxima)
    total = None
    for b, m in zip(blocks, maxima):
        s = jnp.broadcast_to(jnp.exp2(m - top), b.shape)
        if part == 2:
            s = jnp.where((lane >= F_LANE) & (lane < L_LANE), 1.0, s)
        total = b * s if total is None else total + b * s
    return jnp.where(lane == M_LANE, top, total)


def kernel(
    dims,
    col0,
    q_ref,
    slab_ref,
    groups_ref,
    own_ref,
    row_ref,
    out_ref,
    pre_v,
    slab_v,
    x_buf,
    f0,
    f1,
    f2,
    sel_buf,
    idx_v,
    idx_s,
    rows_buf,
    logits,
    tops,
    pay,
    got0,
    mid0,
    got1,
    mid1,
    got2,
    mid2,
    got3,
    lsem,
    xs,
    xr,
    fs,
    fr,
    s0,
    r0,
    rs,
    rr,
):
    width = q_ref.shape[1]
    r_dev = slab_ref.shape[0]
    ii, qq = lax.axis_index("index"), lax.axis_index("query")
    coord = (lax.div(ii, dims[1]), lax.rem(ii, dims[1]), lax.div(qq, 2))
    core = lax.rem(qq, 2)
    me_f = (ii * (dims[2] * 2) + qq).astype(F32)
    n = dims[0]
    pairs = n // 2
    k_count = row_ref.shape[1]
    box = (2, n, n, QB, LANES)
    chunk = 2 * n * n * QB
    n_slot = chunk // QB * SLOTS
    f_bufs = (f0, f1, f2)
    x_bufs = [x_buf.at[p] for p in range(3)]

    def device(at, c):
        return (at[0] * n + at[1], at[2] * 2 + c)

    def peer(axis, k):
        at = list(coord)
        at[axis] = lax.rem(coord[axis] + k, n)
        return tuple(at)

    sibling = device(coord, 1 - core)

    pre_copy = pltpu.make_async_copy(slab_ref.at[:, pl.ds(0, PREFIX)], pre_v, lsem.at[0])
    rest_copy = pltpu.make_async_copy(groups_ref, slab_v, lsem.at[1])

    barrier = pltpu.get_barrier_semaphore()
    pl.semaphore_signal(barrier, inc=1, device_id=sibling, device_id_type=pl.DeviceIdType.MESH)
    for axis in range(3):
        for k in range(1, n):
            pl.semaphore_signal(
                barrier, inc=1, device_id=device(peer(axis, k), core), device_id_type=pl.DeviceIdType.MESH
            )
    pre_copy.start()
    rest_copy.start()

    here = coord + (core,)
    x_buf[(0,) + here] = q_ref[:, 0:LANES]
    x_buf[(1,) + here] = q_ref[:, LANES:PREFIX]
    row = row_ref[...]
    numbers = jnp.concatenate(
        [
            own_ref[...].astype(F32),
            lax.shift_right_logical(row, 6).astype(F32),
            (row & 63).astype(F32),
            jnp.zeros((QB, LANES - 3 * k_count), F32),
        ],
        axis=1,
    )
    x_buf[(2,) + here] = numbers.astype(BF16)
    for p in range(3):
        f_bufs[p][here] = q_ref[:, col0[p] : col0[p + 1]]
    pl.semaphore_wait(barrier, 1 + 3 * (n - 1))

    def send(src, dst, ssem, rsem, target):
        pltpu.make_async_remote_copy(
            src_ref=src,
            dst_ref=dst,
            send_sem=ssem,
            recv_sem=rsem,
            device_id=target,
            device_id_type=pl.DeviceIdType.MESH,
        ).start()

    def wait_bytes(ref, sem):
        pltpu.make_async_copy(ref, ref, sem).wait()

    def phase_box(phase):
        if phase == 3:
            return (slice(None),) * 3 + (0,)
        return (slice(0, n - 1),) + (slice(None),) * phase + (0,) * (2 - phase) + (0,)

    def gather_start(bufs, ssem_of, rsem, phase, p):
        if phase == 3:
            block = bufs[p].at[:, :, :, core]
            targets = [sibling]
        else:
            done = ORDERS[p][:phase]
            where = tuple(slice(None) if a in done else coord[a] for a in range(3))
            block = bufs[p].at[where + (core,)]
            axis = ORDERS[p][phase]
            targets = [device(peer(axis, k), core) for k in range(1, n)]
        for target in targets:
            send(block, block, ssem_of(p, phase), rsem.at[p * 4 + phase], target)

    def x_ssem(p, phase):
        return xs.at[phase]

    def f_ssem(p, phase):
        return fs.at[p * 4 + phase]

    def x_start(phase):
        for p in range(3):
            gather_start(x_bufs, x_ssem, xr, phase, p)

    def f_start(phase):
        for p in range(3):
            gather_start(f_bufs, f_ssem, fr, phase, p)

    def x_step(phase):
        for p in range(3):
            wait_bytes(x_bufs[p].at[phase_box(phase)], xr.at[p * 4 + phase])
            if phase < 3:
                gather_start(x_bufs, x_ssem, xr, phase + 1, p)

    def f_step(phase):
        for p in range(3):
            wait_bytes(f_bufs[p].at[phase_box(phase)], fr.at[p * 4 + phase])
            if phase < 3:
                gather_start(f_bufs, f_ssem, fr, phase + 1, p)

    x_start(0)
    f_start(0)
    x_step(0)
    x_step(1)
    f_step(0)
    x_step(2)
    f_step(1)

    def part_of(buf, t, c):
        v = buf[pl.ds(2 * t, 2), :, :, c]
        return v.astype(F32).reshape(chunk, v.shape[-1])

    def index(j, t, c):
        numbers = part_of(x_bufs[2], t, c)
        lane = lane_of(chunk)
        hit = (numbers == me_f) & (lane < k_count)
        high = pltpu.roll(numbers, LANES - k_count, 1)
        low = pltpu.roll(numbers, LANES - 2 * k_count, 1)
        any_hit = jnp.sum(jnp.where(hit, 1.0, 0.0), axis=1, keepdims=True)
        high = jnp.sum(jnp.where(hit, high, 0.0), axis=1, keepdims=True)
        low = jnp.sum(jnp.where(hit, low, 0.0), axis=1, keepdims=True)
        qi = lax.broadcasted_iota(jnp.int32, (chunk, chunk), 0)
        qj = lax.broadcasted_iota(jnp.int32, (chunk, chunk), 1)
        before = jnp.where(((qi >> 3) == (qj >> 3)) & (qj < qi), 1.0, 0.0).astype(BF16)
        rank = jnp.dot(
            before,
            jnp.broadcast_to(any_hit, (chunk, LANES)).astype(BF16),
            preferred_element_type=F32,
        )[:, 0:1]
        rank = jnp.where(any_hit > 0.0, rank, -1.0)
        q_of = lax.broadcasted_iota(jnp.int32, (chunk, n_slot), 0)
        s_of = lax.broadcasted_iota(jnp.int32, (chunk, n_slot), 1)
        sel = jnp.where(
            ((q_of >> 3) == (s_of >> 2)) & (rank == (s_of & 3).astype(F32)), 1.0, 0.0
        )
        sel_buf[j] = sel
        picked = jnp.dot(
            jnp.where(lane < 64, high, low).T.astype(BF16),
            sel.astype(BF16),
            preferred_element_type=F32,
        )
        row_of = (picked[0:1, :] * 64.0 + picked[64:65, :]).astype(jnp.int32)
        idx_v[pl.ds(j, 1), 0:n_slot] = row_of

    def half_of(j):
        return lax.rem(j, pairs), jnp.where(j < pairs, core, 1 - core)

    @pl.loop(0, n)
    def _(j):
        @pl.when(j == pairs)
        def _():
            x_step(3)

        index(j, *half_of(j))

    idx_copy = pltpu.make_async_copy(idx_v, idx_s, lsem.at[2])
    idx_copy.start()
    pre_copy.wait()

    factor = PREFIX ** (-0.5) * math.log2(math.e)
    tile = 512

    def prefix_of(j):
        t, c = half_of(j)
        return jnp.concatenate([part_of(x_bufs[0], t, c), part_of(x_bufs[1], t, c)], axis=1).astype(BF16)

    @pl.loop(0, n)
    def _(j):
        q = prefix_of(j)
        most = jnp.full((chunk, LANES), -jnp.inf, F32)
        for u in range(r_dev // tile):
            s = lax.dot_general(
                q, pre_v[u * tile : (u + 1) * tile, :], NT, preferred_element_type=F32
            )
            logits[j, :, u * tile : (u + 1) * tile] = s
            for v in range(tile // LANES):
                most = jnp.maximum(most, s[:, v * LANES : (v + 1) * LANES])
        tops[j] = jnp.broadcast_to(jnp.max(most, axis=1, keepdims=True) * factor, (chunk, LANES))

    idx_copy.wait()
    rest_copy.wait()

    @pl.loop(0, n * n_slot // QB)
    def _(g):
        sub = lax.broadcasted_iota(jnp.int32, (QB, width), 0)
        rows = jnp.zeros((QB, width), F32)
        for k in range(QB):
            at = g * QB + k
            i = jnp.clip(idx_s[lax.div(at, n_slot), lax.rem(at, n_slot)], 0, r_dev - 1)
            group = slab_v[i >> 3].astype(F32)
            rows = jnp.where(sub == k, pltpu.roll(group, (k - (i & 7)) & 7, 0), rows)
        rows_buf[g] = rows

    f_step(2)

    @pl.loop(0, n)
    def _(jj):
        j = lax.rem(jj + pairs, n)
        top = tops[j][:, 0:1]
        total = jnp.zeros((chunk, LANES), F32)
        acc = jnp.zeros((chunk, PREFIX), F32)
        for u in range(r_dev // tile):
            w = jnp.exp2(logits[j, :, u * tile : (u + 1) * tile] * factor - top)
            for v in range(tile // LANES):
                total = total + w[:, v * LANES : (v + 1) * LANES]
            acc = acc + jnp.dot(
                w.astype(BF16), pre_v[u * tile : (u + 1) * tile, :], preferred_element_type=F32
            )
        total = jnp.sum(total, axis=1, keepdims=True)
        lane = lane_of(chunk)
        p0, p1 = acc[:, :LANES], acc[:, LANES:]
        b = jnp.where(lane < 32, pltpu.roll(p0, 32, 1), pltpu.roll(p1, 32, 1))
        c = jnp.where(lane < F_LANE, pltpu.roll(p1, 64, 1), 0.0)
        c = jnp.where(lane == L_LANE, total, c)
        for p, v in enumerate((p0, b, c)):
            pay[j, p] = jnp.where(lane == M_LANE, top, v).reshape(box)

        @pl.when(jj < pairs)
        def _():
            send(pay.at[j, pl.ds(0, 2)], got0.at[jj, pl.ds(0, 2)], s0.at[jj], r0.at[jj], sibling)

    f_step(3)

    @pl.loop(0, n)
    def _(jj):
        j = lax.rem(jj + pairs, n)
        t, c = half_of(j)
        groups = pl.ds(j * (n_slot // QB), n_slot // QB)

        def rows_of(lo, hi):
            return rows_buf[groups, :, lo:hi].reshape(n_slot, hi - lo).astype(BF16)

        scores = lax.dot_general(prefix_of(j), rows_of(0, PREFIX), NT, preferred_element_type=F32)
        for p in range(3):
            scores = scores + lax.dot_general(
                part_of(f_bufs[p], t, c).astype(BF16),
                rows_of(col0[p], col0[p + 1]),
                NT,
                preferred_element_type=F32,
            )
        full = jnp.sum(scores * sel_buf[j], axis=1, keepdims=True)
        lane = lane_of(chunk)
        full = jnp.where((part_of(x_bufs[2], t, c) == me_f) & (lane < k_count), full, 0.0)
        pay[j, 2] = pay[j, 2] + pltpu.roll(full, F_LANE, 1).reshape(box)

        @pl.when(jj < pairs)
        def _():
            send(pay.at[j, 2], got0.at[jj, 2], s0.at[pairs + jj], r0.at[pairs + jj], sibling)

    def at_axis(axes, axis, index):
        return tuple(index if a == axis else slice(None) for a in axes)

    for p in range(3):

        @pl.loop(0, pairs)
        def _(t, p=p):
            if p == 0:
                wait_bytes(got0.at[t, pl.ds(0, 2)], r0.at[t])
            elif p == 2:
                wait_bytes(got0.at[t, 2], r0.at[pairs + t])
            both = merge(p, [pay[t, p].reshape(chunk, LANES), got0[t, p].reshape(chunk, LANES)])
            mid0[p, pl.ds(2 * t, 2)] = both.reshape(box)

        axis = ORDERS[p][0]
        for k in range(1, n):
            to = peer(axis, k)
            send(mid0.at[(p,) + at_axis(range(3), axis, to[axis])], got1.at[p, k - 1], rs.at[0], rr.at[p], device(to, core))

    flat1 = (n * n * QB, LANES)
    for p in range(3):
        wait_bytes(got1.at[p], rr.at[p])
        first, second, third = ORDERS[p]
        own = mid0[(p,) + at_axis(range(3), first, coord[first])].reshape(flat1)
        blocks = [own] + [got1[p, k - 1].reshape(flat1) for k in range(1, n)]
        mid1[p] = merge(p, blocks).reshape(n, n, QB, LANES)
        left = [a for a in range(3) if a != first]
        for k in range(1, n):
            to = peer(second, k)
            send(mid1.at[(p,) + at_axis(left, second, to[second])], got2.at[p, k - 1], rs.at[1], rr.at[3 + p], device(to, core))

    flat2 = (n * QB, LANES)
    for p in range(3):
        wait_bytes(got2.at[p], rr.at[3 + p])
        first, second, third = ORDERS[p]
        left = [a for a in range(3) if a != first]
        own = mid1[(p,) + at_axis(left, second, coord[second])].reshape(flat2)
        blocks = [own] + [got2[p, k - 1].reshape(flat2) for k in range(1, n)]
        mid2[p] = merge(p, blocks).reshape(n, QB, LANES)
        for k in range(1, n):
            to = peer(third, k)
            send(mid2.at[p, to[third]], got3.at[p, k - 1], rs.at[2], rr.at[6 + p], device(to, core))

    out = []
    for p in range(3):
        wait_bytes(got3.at[p], rr.at[6 + p])
        own = mid2[p, coord[ORDERS[p][2]]]
        out.append(merge(p, [own] + [got3[p, k - 1] for k in range(1, n)]))

    lane = lane_of(QB)
    a, b, c = out
    total = c[:, L_LANE : L_LANE + 1]
    b_back = pltpu.roll(b, 96, 1)
    out_ref[:, 0:LANES] = jnp.where(lane < 96, a, b_back) / total
    out_ref[:, LANES:PREFIX] = jnp.where(lane < 64, b_back, pltpu.roll(c, 64, 1)) / total
    lse = c[:, M_LANE:] * math.log(2.0) + jnp.log(total)
    full = pltpu.roll(c, LANES - F_LANE, 1) * width ** (-0.5)
    out_ref[:, PREFIX : PREFIX + LANES] = full - lse
    out_ref[:, PREFIX + LANES :] = jnp.broadcast_to(lse, (QB, LANES))

    for phase in range(4):
        wait_bytes(x_buf.at[(slice(None),) + phase_box(phase)], xs.at[phase])
        for p in range(3):
            wait_bytes(f_bufs[p].at[phase_box(phase)], fs.at[p * 4 + phase])
    for t in range(pairs):
        wait_bytes(got0.at[t, pl.ds(0, 2)], s0.at[t])
        wait_bytes(got0.at[t, 2], s0.at[pairs + t])
    wait_bytes(got1, rs.at[0])
    wait_bytes(got2, rs.at[1])
    wait_bytes(got3, rs.at[2])


def split(in_ref, pooled_ref, lse_ref, margin_ref):
    pooled_ref[...] = in_ref[:, 0:PREFIX]
    margin_ref[...] = in_ref[:, PREFIX : PREFIX + margin_ref.shape[1]]
    here = lax.broadcasted_iota(jnp.int32, (QB, LANES), 0) == lane_of(QB)
    lse = jnp.sum(jnp.where(here, in_ref[:, PREFIX + LANES :], 0.0), axis=0, keepdims=True)
    lse_ref[...] = lse[:, 0:QB]


def make(mesh, dims):
    def on_device(queries, slab, cand_owner, cand_row):
        width = queries.shape[1]
        r_dev = slab.shape[0]
        k_count = cand_owner.shape[1]
        tiles = (width - PREFIX) // LANES
        n0 = -(-tiles // 3)
        n1 = -(-(tiles - n0) // 2)
        col0 = (PREFIX, PREFIX + n0 * LANES, PREFIX + (n0 + n1) * LANES, width)
        n = dims[0]
        chunk = 2 * n * n * QB
        n_slot = chunk // QB * SLOTS
        vmem = pltpu.VMEM
        dma = pltpu.SemaphoreType.DMA
        spec = pl.BlockSpec(memory_space=pltpu.VMEM)
        merged = pl.pallas_call(
            functools.partial(kernel, dims, col0),
            out_shape=jax.ShapeDtypeStruct((QB, PREFIX + 2 * LANES), F32),
            in_specs=[spec, pl.BlockSpec(memory_space=pl.ANY), pl.BlockSpec(memory_space=pl.ANY), spec, spec],
            out_specs=spec,
            scratch_shapes=[
                vmem((r_dev, PREFIX), BF16),
                vmem((r_dev // QB, QB, width), BF16),
                vmem((3, n, n, n, 2, QB, LANES), BF16),
                vmem((n, n, n, 2, QB, col0[1] - col0[0]), BF16),
                vmem((n, n, n, 2, QB, col0[2] - col0[1]), BF16),
                vmem((n, n, n, 2, QB, col0[3] - col0[2]), BF16),
                vmem((n, chunk, n_slot), F32),
                vmem((QB, LANES), jnp.int32),
                pltpu.SMEM((QB, LANES), jnp.int32),
                vmem((n * n_slot // QB, QB, width), F32),
                vmem((n, chunk, r_dev), F32),
                vmem((n, chunk, LANES), F32),
                vmem((n, 3) + (2, n, n, QB, LANES), F32),
                vmem((n // 2, 3) + (2, n, n, QB, LANES), F32),
                vmem((3, n, n, n, QB, LANES), F32),
                vmem((3, n - 1, n, n, QB, LANES), F32),
                vmem((3, n, n, QB, LANES), F32),
                vmem((3, n - 1, n, QB, LANES), F32),
                vmem((3, n, QB, LANES), F32),
                vmem((3, n - 1, QB, LANES), F32),
                dma((3,)),
                dma((4,)),
                dma((12,)),
                dma((12,)),
                dma((12,)),
                dma((n,)),
                dma((n,)),
                dma((3,)),
                dma((9,)),
            ],
            compiler_params=pltpu.CompilerParams(
                collective_id=0, has_side_effects=True, vmem_limit_bytes=56 * 2**20
            ),
        )(queries, slab, slab.reshape(r_dev // QB, QB, width), cand_owner, cand_row)
        pooled, lse, margin = pl.pallas_call(
            split,
            out_shape=(
                jax.ShapeDtypeStruct((QB, PREFIX), F32),
                jax.ShapeDtypeStruct((1, QB), F32),
                jax.ShapeDtypeStruct((QB, k_count), F32),
            ),
            in_specs=[spec],
            out_specs=(spec, spec, spec),
        )(merged)
        return pooled, lse.reshape(QB), margin

    both = ("index", "query")
    return jax.shard_map(
        on_device,
        mesh=mesh,
        in_specs=(P(both, None),) * 4,
        out_specs=(P(both, None), P(both), P(both, None)),
        check_vma=False,
    )


def solution(mesh):
    side = math.isqrt(mesh.shape["index"])
    return make(mesh, (side, side, mesh.shape["query"] // 2))
```

```python
import functools
import math

import jax
import jax.numpy as jnp
from jax import lax
from jax.experimental import pallas as pl
from jax.experimental.pallas import tpu as pltpu
from jax.sharding import PartitionSpec as P

PREFIX = 256
LANES = 128
QB = 8
SLOTS = 4
F32 = jnp.float32
BF16 = jnp.bfloat16
ORDERS = ((1, 0, 2), (0, 2, 1), (2, 1, 0))
NT = (((1,), (1,)), ((), ()))
M_LANE = 127
L_LANE = 96
F_LANE = 64


def lane_of(rows):
    return lax.broadcasted_iota(jnp.int32, (rows, LANES), 1)


def merge(part, blocks):
    lane = lane_of(blocks[0].shape[0])
    maxima = [b[:, M_LANE:] for b in blocks]
    top = functools.reduce(jnp.maximum, maxima)
    total = None
    for b, m in zip(blocks, maxima):
        s = jnp.broadcast_to(jnp.exp2(m - top), b.shape)
        if part == 2:
            s = jnp.where((lane >= F_LANE) & (lane < L_LANE), 1.0, s)
        total = b * s if total is None else total + b * s
    return jnp.where(lane == M_LANE, top, total)


def kernel(
    dims,
    col0,
    q_ref,
    slab_ref,
    groups_ref,
    own_ref,
    row_ref,
    out_ref,
    pre_v,
    slab_v,
    x_buf,
    f0,
    f1,
    f2,
    sel_buf,
    sel_got,
    idx_v,
    idx_s,
    rows_buf,
    rows_got,
    logits,
    tops,
    pay,
    got0,
    mid0,
    got1,
    mid1,
    got2,
    mid2,
    got3,
    lsem,
    xs,
    xr,
    fs,
    fr,
    ws,
    wr,
    s0,
    r0,
    rs,
    rr,
):
    width = q_ref.shape[1]
    r_dev = slab_ref.shape[0]
    ii, qq = lax.axis_index("index"), lax.axis_index("query")
    coord = (lax.div(ii, dims[1]), lax.rem(ii, dims[1]), lax.div(qq, 2))
    core = lax.rem(qq, 2)
    me_f = (ii * (dims[2] * 2) + qq).astype(F32)
    n = dims[0]
    pairs = n // 2
    k_count = row_ref.shape[1]
    box = (2, n, n, QB, LANES)
    chunk = 2 * n * n * QB
    n_slot = chunk // QB * SLOTS
    f_bufs = (f0, f1, f2)
    x_bufs = [x_buf.at[p] for p in range(3)]

    def device(at, c):
        return (at[0] * n + at[1], at[2] * 2 + c)

    def peer(axis, k):
        at = list(coord)
        at[axis] = lax.rem(coord[axis] + k, n)
        return tuple(at)

    sibling = device(coord, 1 - core)

    pre_copy = pltpu.make_async_copy(slab_ref.at[:, pl.ds(0, PREFIX)], pre_v, lsem.at[0])
    rest_copy = pltpu.make_async_copy(groups_ref, slab_v, lsem.at[1])

    barrier = pltpu.get_barrier_semaphore()
    pl.semaphore_signal(barrier, inc=1, device_id=sibling, device_id_type=pl.DeviceIdType.MESH)
    for axis in range(3):
        for k in range(1, n):
            pl.semaphore_signal(
                barrier, inc=1, device_id=device(peer(axis, k), core), device_id_type=pl.DeviceIdType.MESH
            )
    pre_copy.start()
    rest_copy.start()

    here = coord + (core,)
    x_buf[(0,) + here] = q_ref[:, 0:LANES]
    x_buf[(1,) + here] = q_ref[:, LANES:PREFIX]
    row = row_ref[...]
    numbers = jnp.concatenate(
        [
            own_ref[...].astype(F32),
            lax.shift_right_logical(row, 6).astype(F32),
            (row & 63).astype(F32),
            jnp.zeros((QB, LANES - 3 * k_count), F32),
        ],
        axis=1,
    )
    x_buf[(2,) + here] = numbers.astype(BF16)
    for p in range(3):
        f_bufs[p][coord] = q_ref[:, col0[p] : col0[p + 1]]
    pl.semaphore_wait(barrier, 1 + 3 * (n - 1))

    def send(src, dst, ssem, rsem, target):
        pltpu.make_async_remote_copy(
            src_ref=src,
            dst_ref=dst,
            send_sem=ssem,
            recv_sem=rsem,
            device_id=target,
            device_id_type=pl.DeviceIdType.MESH,
        ).start()

    def wait_bytes(ref, sem):
        pltpu.make_async_copy(ref, ref, sem).wait()

    def phase_box(phase):
        if phase == 3:
            return (slice(None),) * 3
        return (slice(0, n - 1),) + (slice(None),) * phase + (0,) * (2 - phase)

    def gather_start(buf, tail, ssem, rsem, phase, p):
        if phase == 3:
            block = buf.at[(slice(None),) * 3 + tail]
            targets = [sibling]
        else:
            done = ORDERS[p][:phase]
            where = tuple(slice(None) if a in done else coord[a] for a in range(3))
            block = buf.at[where + tail]
            axis = ORDERS[p][phase]
            targets = [device(peer(axis, k), core) for k in range(1, n)]
        for target in targets:
            send(block, block, ssem, rsem, target)

    def x_start(phase, p):
        gather_start(x_bufs[p], (core,), xs.at[phase], xr.at[p * 4 + phase], phase, p)

    def f_start(phase, p):
        gather_start(f_bufs[p], (), fs.at[p * 3 + phase], fr.at[p * 3 + phase], phase, p)

    def x_step(phase):
        for p in range(3):
            wait_bytes(x_bufs[p].at[phase_box(phase) + (0,)], xr.at[p * 4 + phase])
            if phase < 3:
                x_start(phase + 1, p)

    def f_step(phase):
        for p in range(3):
            wait_bytes(f_bufs[p].at[phase_box(phase)], fr.at[p * 3 + phase])
            if phase < 2:
                f_start(phase + 1, p)

    for p in range(3):
        x_start(0, p)
    for p in range(3):
        f_start(0, p)
    x_step(0)
    x_step(1)
    f_step(0)
    x_step(2)
    f_step(1)

    def part_of(buf, t, *c):
        v = buf[(pl.ds(2 * t, 2), slice(None), slice(None)) + c]
        return v.astype(F32).reshape(chunk, v.shape[-1])

    def index(j, t, c):
        numbers = part_of(x_bufs[2], t, c)
        lane = lane_of(chunk)
        hit = (numbers == me_f) & (lane < k_count)
        high = pltpu.roll(numbers, LANES - k_count, 1)
        low = pltpu.roll(numbers, LANES - 2 * k_count, 1)
        any_hit = jnp.sum(jnp.where(hit, 1.0, 0.0), axis=1, keepdims=True)
        high = jnp.sum(jnp.where(hit, high, 0.0), axis=1, keepdims=True)
        low = jnp.sum(jnp.where(hit, low, 0.0), axis=1, keepdims=True)
        qi = lax.broadcasted_iota(jnp.int32, (chunk, chunk), 0)
        qj = lax.broadcasted_iota(jnp.int32, (chunk, chunk), 1)
        before = jnp.where(((qi >> 3) == (qj >> 3)) & (qj < qi), 1.0, 0.0).astype(BF16)
        rank = jnp.dot(
            before,
            jnp.broadcast_to(any_hit, (chunk, LANES)).astype(BF16),
            preferred_element_type=F32,
        )[:, 0:1]
        rank = jnp.where(any_hit > 0.0, rank, -1.0)
        q_of = lax.broadcasted_iota(jnp.int32, (chunk, n_slot), 0)
        s_of = lax.broadcasted_iota(jnp.int32, (chunk, n_slot), 1)
        sel = jnp.where(
            ((q_of >> 3) == (s_of >> 2)) & (rank == (s_of & 3).astype(F32)), 1.0, 0.0
        )
        sel_buf[j] = sel
        picked = jnp.dot(
            jnp.where(lane < 64, high, low).T.astype(BF16),
            sel.astype(BF16),
            preferred_element_type=F32,
        )
        row_of = (picked[0:1, :] * 64.0 + picked[64:65, :]).astype(jnp.int32)
        idx_v[pl.ds(j, 1), 0:n_slot] = row_of

    def half_of(j):
        return lax.rem(j, pairs), jnp.where(j < pairs, core, 1 - core)

    @pl.loop(0, n)
    def _(j):
        @pl.when(j == pairs)
        def _():
            x_step(3)

        index(j, *half_of(j))

    idx_copy = pltpu.make_async_copy(idx_v, idx_s, lsem.at[2])
    idx_copy.start()
    send(sel_buf.at[pl.ds(pairs, pairs)], sel_got, ws.at[0], wr.at[0], sibling)
    pre_copy.wait()

    factor = PREFIX ** (-0.5) * math.log2(math.e)
    tile = 512

    def prefix_of(j):
        t, c = half_of(j)
        return jnp.concatenate([part_of(x_bufs[0], t, c), part_of(x_bufs[1], t, c)], axis=1).astype(BF16)

    @pl.loop(0, n)
    def _(j):
        q = prefix_of(j)
        most = jnp.full((chunk, LANES), -jnp.inf, F32)
        for u in range(r_dev // tile):
            s = lax.dot_general(
                q, pre_v[u * tile : (u + 1) * tile, :], NT, preferred_element_type=F32
            )
            logits[j, :, u * tile : (u + 1) * tile] = s
            for v in range(tile // LANES):
                most = jnp.maximum(most, s[:, v * LANES : (v + 1) * LANES])
        tops[j] = jnp.broadcast_to(jnp.max(most, axis=1, keepdims=True) * factor, (chunk, LANES))

    idx_copy.wait()
    rest_copy.wait()

    half = pairs * n_slot // QB

    @pl.loop(0, 2)
    def _(h):
        @pl.loop(0, half)
        def _(gg):
            g = (1 - h) * half + gg
            sub = lax.broadcasted_iota(jnp.int32, (QB, width), 0)
            rows = jnp.zeros((QB, width), F32)
            for k in range(QB):
                at = g * QB + k
                i = jnp.clip(idx_s[lax.div(at, n_slot), lax.rem(at, n_slot)], 0, r_dev - 1)
                group = slab_v[i >> 3].astype(F32)
                rows = jnp.where(sub == k, pltpu.roll(group, (k - (i & 7)) & 7, 0), rows)
            rows_buf[g] = rows.astype(BF16)

        @pl.when(h == 0)
        def _():
            send(rows_buf.at[pl.ds(half, half)], rows_got, ws.at[1], wr.at[1], sibling)

    @pl.loop(0, n)
    def _(jj):
        j = lax.rem(jj + pairs, n)
        top = tops[j][:, 0:1]
        total = jnp.zeros((chunk, LANES), F32)
        acc = jnp.zeros((chunk, PREFIX), F32)
        for u in range(r_dev // tile):
            w = jnp.exp2(logits[j, :, u * tile : (u + 1) * tile] * factor - top)
            for v in range(tile // LANES):
                total = total + w[:, v * LANES : (v + 1) * LANES]
            acc = acc + jnp.dot(
                w.astype(BF16), pre_v[u * tile : (u + 1) * tile, :], preferred_element_type=F32
            )
        total = jnp.sum(total, axis=1, keepdims=True)
        lane = lane_of(chunk)
        p0, p1 = acc[:, :LANES], acc[:, LANES:]
        b = jnp.where(lane < 32, pltpu.roll(p0, 32, 1), pltpu.roll(p1, 32, 1))
        c = jnp.where(lane < F_LANE, pltpu.roll(p1, 64, 1), 0.0)
        c = jnp.where(lane == L_LANE, total, c)
        for p, v in enumerate((p0, b, c)):
            pay[j, p] = jnp.where(lane == M_LANE, top, v).reshape(box)

        @pl.when(jj < pairs)
        def _():
            send(pay.at[j], got0.at[jj], s0.at[jj], r0.at[jj], sibling)

    f_step(2)
    wait_bytes(sel_got, wr.at[0])
    wait_bytes(rows_got, wr.at[1])

    sibling_f = me_f + (1 - 2 * core).astype(F32)
    step = n_slot // QB

    @pl.loop(0, pairs)
    def _(t):
        def rows_of(lo, hi):
            groups = pl.ds(t * step, step)
            mine = rows_buf[groups, :, lo:hi].astype(F32).reshape(n_slot, hi - lo)
            other = rows_got[groups, :, lo:hi].astype(F32).reshape(n_slot, hi - lo)
            return jnp.concatenate([mine, other], axis=0).astype(BF16)

        scores = lax.dot_general(prefix_of(t), rows_of(0, PREFIX), NT, preferred_element_type=F32)
        for p in range(3):
            scores = scores + lax.dot_general(
                part_of(f_bufs[p], t).astype(BF16),
                rows_of(col0[p], col0[p + 1]),
                NT,
                preferred_element_type=F32,
            )
        lane = lane_of(chunk)
        numbers = jnp.where(lane < k_count, part_of(x_bufs[2], t, core), -1.0)
        full = jnp.sum(scores[:, :n_slot] * sel_buf[t], axis=1, keepdims=True)
        full2 = jnp.sum(scores[:, n_slot:] * sel_got[t], axis=1, keepdims=True)
        full = jnp.where(numbers == me_f, full, jnp.where(numbers == sibling_f, full2, 0.0))
        pay[t, 2] = pay[t, 2] + pltpu.roll(full, F_LANE, 1).reshape(box)

    def at_axis(axes, axis, index):
        return tuple(index if a == axis else slice(None) for a in axes)

    for p in range(3):

        @pl.loop(0, pairs)
        def _(t, p=p):
            if p == 0:
                wait_bytes(got0.at[t], r0.at[t])
            both = merge(p, [pay[t, p].reshape(chunk, LANES), got0[t, p].reshape(chunk, LANES)])
            mid0[p, pl.ds(2 * t, 2)] = both.reshape(box)

        axis = ORDERS[p][0]
        for k in range(1, n):
            to = peer(axis, k)
            send(mid0.at[(p,) + at_axis(range(3), axis, to[axis])], got1.at[p, k - 1], rs.at[0], rr.at[p], device(to, core))

    flat1 = (n * n * QB, LANES)
    for p in range(3):
        wait_bytes(got1.at[p], rr.at[p])
        first, second, third = ORDERS[p]
        own = mid0[(p,) + at_axis(range(3), first, coord[first])].reshape(flat1)
        blocks = [own] + [got1[p, k - 1].reshape(flat1) for k in range(1, n)]
        mid1[p] = merge(p, blocks).reshape(n, n, QB, LANES)
        left = [a for a in range(3) if a != first]
        for k in range(1, n):
            to = peer(second, k)
            send(mid1.at[(p,) + at_axis(left, second, to[second])], got2.at[p, k - 1], rs.at[1], rr.at[3 + p], device(to, core))

    flat2 = (n * QB, LANES)
    for p in range(3):
        wait_bytes(got2.at[p], rr.at[3 + p])
        first, second, third = ORDERS[p]
        left = [a for a in range(3) if a != first]
        own = mid1[(p,) + at_axis(left, second, coord[second])].reshape(flat2)
        blocks = [own] + [got2[p, k - 1].reshape(flat2) for k in range(1, n)]
        mid2[p] = merge(p, blocks).reshape(n, QB, LANES)
        for k in range(1, n):
            to = peer(third, k)
            send(mid2.at[p, to[third]], got3.at[p, k - 1], rs.at[2], rr.at[6 + p], device(to, core))

    out = []
    for p in range(3):
        wait_bytes(got3.at[p], rr.at[6 + p])
        own = mid2[p, coord[ORDERS[p][2]]]
        out.append(merge(p, [own] + [got3[p, k - 1] for k in range(1, n)]))

    lane = lane_of(QB)
    a, b, c = out
    total = c[:, L_LANE : L_LANE + 1]
    b_back = pltpu.roll(b, 96, 1)
    out_ref[:, 0:LANES] = jnp.where(lane < 96, a, b_back) / total
    out_ref[:, LANES:PREFIX] = jnp.where(lane < 64, b_back, pltpu.roll(c, 64, 1)) / total
    lse = c[:, M_LANE:] * math.log(2.0) + jnp.log(total)
    full = pltpu.roll(c, LANES - F_LANE, 1) * width ** (-0.5)
    out_ref[:, PREFIX : PREFIX + LANES] = full - lse
    out_ref[:, PREFIX + LANES :] = jnp.broadcast_to(lse, (QB, LANES))

    for phase in range(4):
        wait_bytes(x_buf.at[(slice(None),) + phase_box(phase) + (0,)], xs.at[phase])
    for phase in range(3):
        for p in range(3):
            wait_bytes(f_bufs[p].at[phase_box(phase)], fs.at[p * 3 + phase])
    wait_bytes(sel_got, ws.at[0])
    wait_bytes(rows_got, ws.at[1])
    for t in range(pairs):
        wait_bytes(got0.at[t], s0.at[t])
    wait_bytes(got1, rs.at[0])
    wait_bytes(got2, rs.at[1])
    wait_bytes(got3, rs.at[2])


def split(in_ref, pooled_ref, lse_ref, margin_ref):
    pooled_ref[...] = in_ref[:, 0:PREFIX]
    margin_ref[...] = in_ref[:, PREFIX : PREFIX + margin_ref.shape[1]]
    here = lax.broadcasted_iota(jnp.int32, (QB, LANES), 0) == lane_of(QB)
    lse = jnp.sum(jnp.where(here, in_ref[:, PREFIX + LANES :], 0.0), axis=0, keepdims=True)
    lse_ref[...] = lse[:, 0:QB]


def make(mesh, dims):
    def on_device(queries, slab, cand_owner, cand_row):
        width = queries.shape[1]
        r_dev = slab.shape[0]
        k_count = cand_owner.shape[1]
        tiles = (width - PREFIX) // LANES
        n0 = -(-tiles // 3)
        n1 = -(-(tiles - n0) // 2)
        col0 = (PREFIX, PREFIX + n0 * LANES, PREFIX + (n0 + n1) * LANES, width)
        n = dims[0]
        chunk = 2 * n * n * QB
        n_slot = chunk // QB * SLOTS
        vmem = pltpu.VMEM
        dma = pltpu.SemaphoreType.DMA
        spec = pl.BlockSpec(memory_space=pltpu.VMEM)
        merged = pl.pallas_call(
            functools.partial(kernel, dims, col0),
            out_shape=jax.ShapeDtypeStruct((QB, PREFIX + 2 * LANES), F32),
            in_specs=[spec, pl.BlockSpec(memory_space=pl.ANY), pl.BlockSpec(memory_space=pl.ANY), spec, spec],
            out_specs=spec,
            scratch_shapes=[
                vmem((r_dev, PREFIX), BF16),
                vmem((r_dev // QB, QB, width), BF16),
                vmem((3, n, n, n, 2, QB, LANES), BF16),
                vmem((n, n, n, QB, col0[1] - col0[0]), BF16),
                vmem((n, n, n, QB, col0[2] - col0[1]), BF16),
                vmem((n, n, n, QB, col0[3] - col0[2]), BF16),
                vmem((n, chunk, n_slot), F32),
                vmem((n // 2, chunk, n_slot), F32),
                vmem((QB, LANES), jnp.int32),
                pltpu.SMEM((QB, LANES), jnp.int32),
                vmem((n * n_slot // QB, QB, width), BF16),
                vmem((n * n_slot // QB // 2, QB, width), BF16),
                vmem((n, chunk, r_dev), F32),
                vmem((n, chunk, LANES), F32),
                vmem((n, 3) + (2, n, n, QB, LANES), F32),
                vmem((n // 2, 3) + (2, n, n, QB, LANES), F32),
                vmem((3, n, n, n, QB, LANES), F32),
                vmem((3, n - 1, n, n, QB, LANES), F32),
                vmem((3, n, n, QB, LANES), F32),
                vmem((3, n - 1, n, QB, LANES), F32),
                vmem((3, n, QB, LANES), F32),
                vmem((3, n - 1, QB, LANES), F32),
                dma((3,)),
                dma((4,)),
                dma((12,)),
                dma((9,)),
                dma((9,)),
                dma((2,)),
                dma((2,)),
                dma((n // 2,)),
                dma((n // 2,)),
                dma((3,)),
                dma((9,)),
            ],
            compiler_params=pltpu.CompilerParams(
                collective_id=0, has_side_effects=True, vmem_limit_bytes=56 * 2**20
            ),
        )(queries, slab, slab.reshape(r_dev // QB, QB, width), cand_owner, cand_row)
        pooled, lse, margin = pl.pallas_call(
            split,
            out_shape=(
                jax.ShapeDtypeStruct((QB, PREFIX), F32),
                jax.ShapeDtypeStruct((1, QB), F32),
                jax.ShapeDtypeStruct((QB, k_count), F32),
            ),
            in_specs=[spec],
            out_specs=(spec, spec, spec),
        )(merged)
        return pooled, lse.reshape(QB), margin

    both = ("index", "query")
    return jax.shard_map(
        on_device,
        mesh=mesh,
        in_specs=(P(both, None),) * 4,
        out_specs=(P(both, None), P(both), P(both, None)),
        check_vma=False,
    )


def solution(mesh):
    side = math.isqrt(mesh.shape["index"])
    return make(mesh, (side, side, mesh.shape["query"] // 2))
```

```python
import functools
import math

import jax
import jax.numpy as jnp
from jax import lax
from jax.experimental import pallas as pl
from jax.experimental.pallas import tpu as pltpu
from jax.sharding import PartitionSpec as P

PREFIX = 256
LANES = 128
QB = 8
SLOTS = 4
F32 = jnp.float32
BF16 = jnp.bfloat16
ORDERS = ((1, 0, 2), (0, 2, 1), (2, 1, 0))
NT = (((1,), (1,)), ((), ()))
M_LANE = 127
L_LANE = 96
F_LANE = 64


def lane_of(rows):
    return lax.broadcasted_iota(jnp.int32, (rows, LANES), 1)


def merge(part, blocks):
    lane = lane_of(blocks[0].shape[0])
    maxima = [b[:, M_LANE:] for b in blocks]
    top = functools.reduce(jnp.maximum, maxima)
    total = None
    for b, m in zip(blocks, maxima):
        s = jnp.broadcast_to(jnp.exp2(m - top), b.shape)
        if part == 2:
            s = jnp.where((lane >= F_LANE) & (lane < L_LANE), 1.0, s)
        total = b * s if total is None else total + b * s
    return jnp.where(lane == M_LANE, top, total)


def kernel(
    dims,
    col0,
    q_ref,
    slab_ref,
    groups_ref,
    own_ref,
    row_ref,
    out_ref,
    pre_v,
    slab_v,
    x_buf,
    f0,
    f1,
    f2,
    sel_buf,
    sel_got,
    idx_v,
    idx_s,
    rows_buf,
    rows_got,
    logits,
    tops,
    pay,
    got0,
    mid0,
    got1,
    mid1,
    got2,
    lsem,
    xs,
    xr,
    fs,
    fr,
    ws,
    wr,
    s0,
    r0,
    rs,
    rr,
):
    width = q_ref.shape[1]
    r_dev = slab_ref.shape[0]
    ii, qq = lax.axis_index("index"), lax.axis_index("query")
    coord = (lax.div(ii, dims[1]), lax.rem(ii, dims[1]), lax.div(qq, 2))
    core = lax.rem(qq, 2)
    me_f = (ii * (dims[2] * 2) + qq).astype(F32)
    n = dims[0]
    pairs = n // 2
    k_count = row_ref.shape[1]
    box = (2, n, n, QB, LANES)
    chunk = 2 * n * n * QB
    n_slot = chunk // QB * SLOTS
    f_bufs = (f0, f1, f2)
    x_bufs = [x_buf.at[p] for p in range(3)]

    def device(at, c):
        return (at[0] * n + at[1], at[2] * 2 + c)

    moved = [[coord[a]] + [lax.rem(coord[a] + k, n) for k in range(1, n)] for a in range(3)]

    def peer(axis, k, axis2=None, k2=0):
        at = list(coord)
        at[axis] = moved[axis][k]
        if axis2 is not None:
            at[axis2] = moved[axis2][k2]
        return tuple(at)

    sibling = device(coord, 1 - core)

    pre_copy = pltpu.make_async_copy(slab_ref.at[:, pl.ds(0, PREFIX)], pre_v, lsem.at[0])
    rest_copy = pltpu.make_async_copy(groups_ref, slab_v, lsem.at[1])

    barrier = pltpu.get_barrier_semaphore()
    pl.semaphore_signal(barrier, inc=1, device_id=sibling, device_id_type=pl.DeviceIdType.MESH)
    near = [peer(a, k) for a in range(3) for k in range(1, n)]
    near += [peer(a, k, b, k2) for a in range(3) for b in range(a) for k in range(1, n) for k2 in range(1, n)]
    for at in near:
        pl.semaphore_signal(
            barrier, inc=1, device_id=device(at, core), device_id_type=pl.DeviceIdType.MESH
        )
    pre_copy.start()
    rest_copy.start()

    here = coord + (core,)
    x_buf[(0,) + here] = q_ref[:, 0:LANES]
    x_buf[(1,) + here] = q_ref[:, LANES:PREFIX]
    row = row_ref[...]
    numbers = jnp.concatenate(
        [
            own_ref[...].astype(F32),
            lax.shift_right_logical(row, 6).astype(F32),
            (row & 63).astype(F32),
            jnp.zeros((QB, LANES - 3 * k_count), F32),
        ],
        axis=1,
    )
    x_buf[(2,) + here] = numbers.astype(BF16)
    for p in range(3):
        f_bufs[p][coord] = q_ref[:, col0[p] : col0[p + 1]]
    pl.semaphore_wait(barrier, 1 + len(near))

    def send(src, dst, ssem, rsem, target):
        pltpu.make_async_remote_copy(
            src_ref=src,
            dst_ref=dst,
            send_sem=ssem,
            recv_sem=rsem,
            device_id=target,
            device_id_type=pl.DeviceIdType.MESH,
        ).start()

    def wait_bytes(ref, sem):
        pltpu.make_async_copy(ref, ref, sem).wait()

    def phase_box(phase):
        if phase == 3:
            return (slice(None),) * 3
        return (slice(0, n - 1),) + (slice(None),) * phase + (0,) * (2 - phase)

    def gather_start(buf, tail, ssem, rsem, phase, p):
        if phase == 3:
            block = buf.at[(slice(None),) * 3 + tail]
            targets = [sibling]
        else:
            done = ORDERS[p][:phase]
            where = tuple(slice(None) if a in done else coord[a] for a in range(3))
            block = buf.at[where + tail]
            axis = ORDERS[p][phase]
            targets = [device(peer(axis, k), core) for k in range(1, n)]
        for target in targets:
            send(block, block, ssem, rsem, target)

    def x_start(phase, p):
        gather_start(x_bufs[p], (core,), xs.at[phase], xr.at[p * 4 + phase], phase, p)

    def f_start(phase, p):
        gather_start(f_bufs[p], (), fs.at[p * 3 + phase], fr.at[p * 3 + phase], phase, p)

    def x_plane(p):
        block = x_bufs[p].at[here]
        first, second = ORDERS[p][:2]
        for k2 in range(n):
            for k in range(0 if k2 else 1, n):
                at = min(k2, 1)
                send(block, block, xs.at[at], xr.at[p * 4 + at], device(peer(first, k, second, k2), core))

    def x_wait(phase, p):
        wait_bytes(x_bufs[p].at[phase_box(phase) + (0,)], xr.at[p * 4 + phase])

    def x_step(phase):
        for p in range(3):
            if phase == 1:
                x_wait(0, p)
            x_wait(phase, p)
            if phase < 3:
                x_start(phase + 1, p)

    def f_step(phase):
        for p in range(3):
            wait_bytes(f_bufs[p].at[phase_box(phase)], fr.at[p * 3 + phase])
            if phase < 2:
                f_start(phase + 1, p)

    for p in range(3):
        x_plane(p)
    for p in range(3):
        f_start(0, p)
    x_step(1)
    f_step(0)
    x_step(2)
    f_step(1)

    def part_of(buf, t, *c):
        v = buf[(pl.ds(2 * t, 2), slice(None), slice(None)) + c]
        return v.astype(F32).reshape(chunk, v.shape[-1])

    def index(j, t, c):
        numbers = part_of(x_bufs[2], t, c)
        lane = lane_of(chunk)
        hit = (numbers == me_f) & (lane < k_count)
        high = pltpu.roll(numbers, LANES - k_count, 1)
        low = pltpu.roll(numbers, LANES - 2 * k_count, 1)
        any_hit = jnp.sum(jnp.where(hit, 1.0, 0.0), axis=1, keepdims=True)
        high = jnp.sum(jnp.where(hit, high, 0.0), axis=1, keepdims=True)
        low = jnp.sum(jnp.where(hit, low, 0.0), axis=1, keepdims=True)
        qi = lax.broadcasted_iota(jnp.int32, (chunk, chunk), 0)
        qj = lax.broadcasted_iota(jnp.int32, (chunk, chunk), 1)
        before = jnp.where(((qi >> 3) == (qj >> 3)) & (qj < qi), 1.0, 0.0).astype(BF16)
        rank = jnp.dot(
            before,
            jnp.broadcast_to(any_hit, (chunk, LANES)).astype(BF16),
            preferred_element_type=F32,
        )[:, 0:1]
        rank = jnp.where(any_hit > 0.0, rank, -1.0)
        q_of = lax.broadcasted_iota(jnp.int32, (chunk, n_slot), 0)
        s_of = lax.broadcasted_iota(jnp.int32, (chunk, n_slot), 1)
        sel = jnp.where(
            ((q_of >> 3) == (s_of >> 2)) & (rank == (s_of & 3).astype(F32)), 1.0, 0.0
        )
        sel_buf[j] = sel
        picked = jnp.dot(
            jnp.where(lane < 64, high, low).T.astype(BF16),
            sel.astype(BF16),
            preferred_element_type=F32,
        )
        row_of = (picked[0:1, :] * 64.0 + picked[64:65, :]).astype(jnp.int32)
        idx_v[pl.ds(j, 1), 0:n_slot] = row_of

    def half_of(j):
        return lax.rem(j, pairs), jnp.where(j < pairs, core, 1 - core)

    @pl.loop(0, n)
    def _(j):
        @pl.when(j == pairs)
        def _():
            x_step(3)

        index(j, *half_of(j))

    idx_copy = pltpu.make_async_copy(idx_v, idx_s, lsem.at[2])
    idx_copy.start()
    send(sel_buf.at[pl.ds(pairs, pairs)], sel_got, ws.at[0], wr.at[0], sibling)
    pre_copy.wait()

    factor = PREFIX ** (-0.5) * math.log2(math.e)
    tile = 512

    def prefix_of(j):
        t, c = half_of(j)
        return jnp.concatenate([part_of(x_bufs[0], t, c), part_of(x_bufs[1], t, c)], axis=1).astype(BF16)

    @pl.loop(0, n)
    def _(j):
        q = prefix_of(j)
        most = jnp.full((chunk, LANES), -jnp.inf, F32)
        for u in range(r_dev // tile):
            s = lax.dot_general(
                q, pre_v[u * tile : (u + 1) * tile, :], NT, preferred_element_type=F32
            )
            logits[j, :, u * tile : (u + 1) * tile] = s
            for v in range(tile // LANES):
                most = jnp.maximum(most, s[:, v * LANES : (v + 1) * LANES])
        tops[j] = jnp.broadcast_to(jnp.max(most, axis=1, keepdims=True) * factor, (chunk, LANES))

    idx_copy.wait()
    rest_copy.wait()

    half = pairs * n_slot // QB

    @pl.loop(0, 2)
    def _(h):
        @pl.loop(0, half)
        def _(gg):
            g = (1 - h) * half + gg
            sub = lax.broadcasted_iota(jnp.int32, (QB, width), 0)
            rows = jnp.zeros((QB, width), F32)
            for k in range(QB):
                at = g * QB + k
                i = jnp.clip(idx_s[lax.div(at, n_slot), lax.rem(at, n_slot)], 0, r_dev - 1)
                group = slab_v[i >> 3].astype(F32)
                rows = jnp.where(sub == k, pltpu.roll(group, (k - (i & 7)) & 7, 0), rows)
            rows_buf[g] = rows.astype(BF16)

        @pl.when(h == 0)
        def _():
            send(rows_buf.at[pl.ds(half, half)], rows_got, ws.at[1], wr.at[1], sibling)

    @pl.loop(0, n)
    def _(jj):
        j = lax.rem(jj + pairs, n)
        top = tops[j][:, 0:1]
        total = jnp.zeros((chunk, LANES), F32)
        acc = jnp.zeros((chunk, PREFIX), F32)
        for u in range(r_dev // tile):
            w = jnp.exp2(logits[j, :, u * tile : (u + 1) * tile] * factor - top)
            for v in range(tile // LANES):
                total = total + w[:, v * LANES : (v + 1) * LANES]
            acc = acc + jnp.dot(
                w.astype(BF16), pre_v[u * tile : (u + 1) * tile, :], preferred_element_type=F32
            )
        total = jnp.sum(total, axis=1, keepdims=True)
        lane = lane_of(chunk)
        p0, p1 = acc[:, :LANES], acc[:, LANES:]
        b = jnp.where(lane < 32, pltpu.roll(p0, 32, 1), pltpu.roll(p1, 32, 1))
        c = jnp.where(lane < F_LANE, pltpu.roll(p1, 64, 1), 0.0)
        c = jnp.where(lane == L_LANE, total, c)
        for p, v in enumerate((p0, b, c)):
            pay[j, p] = jnp.where(lane == M_LANE, top, v).reshape(box)

        @pl.when(jj < pairs)
        def _():
            send(pay.at[j], got0.at[jj], s0.at[jj], r0.at[jj], sibling)

    f_step(2)
    wait_bytes(sel_got, wr.at[0])
    wait_bytes(rows_got, wr.at[1])

    sibling_f = me_f + (1 - 2 * core).astype(F32)
    step = n_slot // QB

    @pl.loop(0, pairs)
    def _(t):
        def rows_of(lo, hi):
            groups = pl.ds(t * step, step)
            mine = rows_buf[groups, :, lo:hi].astype(F32).reshape(n_slot, hi - lo)
            other = rows_got[groups, :, lo:hi].astype(F32).reshape(n_slot, hi - lo)
            return jnp.concatenate([mine, other], axis=0).astype(BF16)

        scores = lax.dot_general(prefix_of(t), rows_of(0, PREFIX), NT, preferred_element_type=F32)
        for p in range(3):
            scores = scores + lax.dot_general(
                part_of(f_bufs[p], t).astype(BF16),
                rows_of(col0[p], col0[p + 1]),
                NT,
                preferred_element_type=F32,
            )
        lane = lane_of(chunk)
        numbers = jnp.where(lane < k_count, part_of(x_bufs[2], t, core), -1.0)
        full = jnp.sum(scores[:, :n_slot] * sel_buf[t], axis=1, keepdims=True)
        full2 = jnp.sum(scores[:, n_slot:] * sel_got[t], axis=1, keepdims=True)
        full = jnp.where(numbers == me_f, full, jnp.where(numbers == sibling_f, full2, 0.0))
        pay[t, 2] = pay[t, 2] + pltpu.roll(full, F_LANE, 1).reshape(box)

    def at_axis(axes, axis, index):
        return tuple(index if a == axis else slice(None) for a in axes)

    for p in range(3):

        @pl.loop(0, pairs)
        def _(t, p=p):
            if p == 0:
                wait_bytes(got0.at[t], r0.at[t])
            both = merge(p, [pay[t, p].reshape(chunk, LANES), got0[t, p].reshape(chunk, LANES)])
            mid0[p, pl.ds(2 * t, 2)] = both.reshape(box)

        axis = ORDERS[p][0]
        for k in range(1, n):
            to = peer(axis, k)
            send(mid0.at[(p,) + at_axis(range(3), axis, to[axis])], got1.at[p, k - 1], rs.at[0], rr.at[p], device(to, core))

    flat1 = (n * n * QB, LANES)
    for p in range(3):
        wait_bytes(got1.at[p], rr.at[p])
        first = ORDERS[p][0]
        own = mid0[(p,) + at_axis(range(3), first, coord[first])].reshape(flat1)
        blocks = [own] + [got1[p, k - 1].reshape(flat1) for k in range(1, n)]
        mid1[p] = merge(p, blocks).reshape(n, n, QB, LANES)
        left = [a for a in range(3) if a != first]
        for k in range(n * n - 1):
            k2, k3 = (k + 1) // n, (k + 1) % n
            to = peer(left[0], k2, left[1], k3)
            send(mid1.at[p, to[left[0]], to[left[1]]], got2.at[p, k], rs.at[1], rr.at[3 + p], device(to, core))

    out = []
    for p in range(3):
        wait_bytes(got2.at[p], rr.at[3 + p])
        left = [coord[a] for a in range(3) if a != ORDERS[p][0]]
        own = mid1[p, left[0], left[1]]
        out.append(merge(p, [own] + [got2[p, k] for k in range(n * n - 1)]))

    lane = lane_of(QB)
    a, b, c = out
    total = c[:, L_LANE : L_LANE + 1]
    b_back = pltpu.roll(b, 96, 1)
    out_ref[:, 0:LANES] = jnp.where(lane < 96, a, b_back) / total
    out_ref[:, LANES:PREFIX] = jnp.where(lane < 64, b_back, pltpu.roll(c, 64, 1)) / total
    lse = c[:, M_LANE:] * math.log(2.0) + jnp.log(total)
    full = pltpu.roll(c, LANES - F_LANE, 1) * width ** (-0.5)
    out_ref[:, PREFIX : PREFIX + LANES] = full - lse
    out_ref[:, PREFIX + LANES :] = jnp.broadcast_to(lse, (QB, LANES))

    for phase in range(4):
        wait_bytes(x_buf.at[(slice(None),) + phase_box(phase) + (0,)], xs.at[phase])
    for phase in range(3):
        for p in range(3):
            wait_bytes(f_bufs[p].at[phase_box(phase)], fs.at[p * 3 + phase])
    wait_bytes(sel_got, ws.at[0])
    wait_bytes(rows_got, ws.at[1])
    for t in range(pairs):
        wait_bytes(got0.at[t], s0.at[t])
    wait_bytes(got1, rs.at[0])
    wait_bytes(got2, rs.at[1])


def split(in_ref, pooled_ref, lse_ref, margin_ref):
    pooled_ref[...] = in_ref[:, 0:PREFIX]
    margin_ref[...] = in_ref[:, PREFIX : PREFIX + margin_ref.shape[1]]
    here = lax.broadcasted_iota(jnp.int32, (QB, LANES), 0) == lane_of(QB)
    lse = jnp.sum(jnp.where(here, in_ref[:, PREFIX + LANES :], 0.0), axis=0, keepdims=True)
    lse_ref[...] = lse[:, 0:QB]


def make(mesh, dims):
    def on_device(queries, slab, cand_owner, cand_row):
        width = queries.shape[1]
        r_dev = slab.shape[0]
        k_count = cand_owner.shape[1]
        tiles = (width - PREFIX) // LANES
        n0 = -(-tiles // 3)
        n1 = -(-(tiles - n0) // 2)
        col0 = (PREFIX, PREFIX + n0 * LANES, PREFIX + (n0 + n1) * LANES, width)
        n = dims[0]
        chunk = 2 * n * n * QB
        n_slot = chunk // QB * SLOTS
        vmem = pltpu.VMEM
        dma = pltpu.SemaphoreType.DMA
        spec = pl.BlockSpec(memory_space=pltpu.VMEM)
        merged = pl.pallas_call(
            functools.partial(kernel, dims, col0),
            out_shape=jax.ShapeDtypeStruct((QB, PREFIX + 2 * LANES), F32),
            in_specs=[spec, pl.BlockSpec(memory_space=pl.ANY), pl.BlockSpec(memory_space=pl.ANY), spec, spec],
            out_specs=spec,
            scratch_shapes=[
                vmem((r_dev, PREFIX), BF16),
                vmem((r_dev // QB, QB, width), BF16),
                vmem((3, n, n, n, 2, QB, LANES), BF16),
                vmem((n, n, n, QB, col0[1] - col0[0]), BF16),
                vmem((n, n, n, QB, col0[2] - col0[1]), BF16),
                vmem((n, n, n, QB, col0[3] - col0[2]), BF16),
                vmem((n, chunk, n_slot), F32),
                vmem((n // 2, chunk, n_slot), F32),
                vmem((QB, LANES), jnp.int32),
                pltpu.SMEM((QB, LANES), jnp.int32),
                vmem((n * n_slot // QB, QB, width), BF16),
                vmem((n * n_slot // QB // 2, QB, width), BF16),
                vmem((n, chunk, r_dev), F32),
                vmem((n, chunk, LANES), F32),
                vmem((n, 3) + (2, n, n, QB, LANES), F32),
                vmem((n // 2, 3) + (2, n, n, QB, LANES), F32),
                vmem((3, n, n, n, QB, LANES), F32),
                vmem((3, n - 1, n, n, QB, LANES), F32),
                vmem((3, n, n, QB, LANES), F32),
                vmem((3, n * n - 1, QB, LANES), F32),
                dma((3,)),
                dma((4,)),
                dma((12,)),
                dma((9,)),
                dma((9,)),
                dma((2,)),
                dma((2,)),
                dma((n // 2,)),
                dma((n // 2,)),
                dma((2,)),
                dma((6,)),
            ],
            compiler_params=pltpu.CompilerParams(
                collective_id=0, has_side_effects=True, vmem_limit_bytes=56 * 2**20
            ),
        )(queries, slab, slab.reshape(r_dev // QB, QB, width), cand_owner, cand_row)
        pooled, lse, margin = pl.pallas_call(
            split,
            out_shape=(
                jax.ShapeDtypeStruct((QB, PREFIX), F32),
                jax.ShapeDtypeStruct((1, QB), F32),
                jax.ShapeDtypeStruct((QB, k_count), F32),
            ),
            in_specs=[spec],
            out_specs=(spec, spec, spec),
        )(merged)
        return pooled, lse.reshape(QB), margin

    both = ("index", "query")
    return jax.shard_map(
        on_device,
        mesh=mesh,
        in_specs=(P(both, None),) * 4,
        out_specs=(P(both, None), P(both), P(both, None)),
        check_vma=False,
    )


def solution(mesh):
    side = math.isqrt(mesh.shape["index"])
    return make(mesh, (side, side, mesh.shape["query"] // 2))
```

```python
import functools
import math

import jax
import jax.numpy as jnp
from jax import lax
from jax.experimental import pallas as pl
from jax.experimental.pallas import tpu as pltpu
from jax.sharding import PartitionSpec as P

PREFIX = 256
LANES = 128
QB = 8
SLOTS = 4
F32 = jnp.float32
BF16 = jnp.bfloat16
ORDERS = ((1, 0, 2), (0, 2, 1), (2, 1, 0))
NT = (((1,), (1,)), ((), ()))
M_LANE = 127
L_LANE = 96
F_LANE = 64


def lane_of(rows):
    return lax.broadcasted_iota(jnp.int32, (rows, LANES), 1)


def merge(part, blocks):
    lane = lane_of(blocks[0].shape[0])
    maxima = [b[:, M_LANE:] for b in blocks]
    top = functools.reduce(jnp.maximum, maxima)
    total = None
    for b, m in zip(blocks, maxima):
        s = jnp.broadcast_to(jnp.exp2(m - top), b.shape)
        if part == 2:
            s = jnp.where((lane >= F_LANE) & (lane < L_LANE), 1.0, s)
        total = b * s if total is None else total + b * s
    return jnp.where(lane == M_LANE, top, total)


def kernel(
    dims,
    col0,
    q_ref,
    slab_ref,
    groups_ref,
    own_ref,
    row_ref,
    out_ref,
    pre_v,
    slab_v,
    x_buf,
    f0,
    f1,
    f2,
    sel_buf,
    sel_got,
    idx_v,
    idx_s,
    rows_buf,
    rows_got,
    logits,
    tops,
    pay,
    got0,
    mid0,
    got1,
    mid1,
    got2,
    lsem,
    xs,
    xr,
    fs,
    fr,
    ws,
    wr,
    s0,
    r0,
    rs,
    rr,
):
    width = q_ref.shape[1]
    r_dev = slab_ref.shape[0]
    ii, qq = lax.axis_index("index"), lax.axis_index("query")
    coord = (lax.div(ii, dims[1]), lax.rem(ii, dims[1]), lax.div(qq, 2))
    core = lax.rem(qq, 2)
    me_f = (ii * (dims[2] * 2) + qq).astype(F32)
    n = dims[0]
    pairs = n // 2
    k_count = row_ref.shape[1]
    box = (2, n, n, QB, LANES)
    chunk = 2 * n * n * QB
    n_slot = chunk // QB * SLOTS
    f_bufs = (f0, f1, f2)
    x_bufs = [x_buf.at[p] for p in range(3)]

    def device(at, c):
        return (at[0] * n + at[1], at[2] * 2 + c)

    moved = [[coord[a]] + [lax.rem(coord[a] + k, n) for k in range(1, n)] for a in range(3)]

    def peer(axis, k, axis2=None, k2=0):
        at = list(coord)
        at[axis] = moved[axis][k]
        if axis2 is not None:
            at[axis2] = moved[axis2][k2]
        return tuple(at)

    sibling = device(coord, 1 - core)
    far_first = sorted(range(1, n), key=lambda k: -min(k, n - k))

    pre_copy = pltpu.make_async_copy(slab_ref.at[:, pl.ds(0, PREFIX)], pre_v, lsem.at[0])
    rest_copy = pltpu.make_async_copy(groups_ref, slab_v, lsem.at[1])

    barrier = pltpu.get_barrier_semaphore()
    pl.semaphore_signal(barrier, inc=1, device_id=sibling, device_id_type=pl.DeviceIdType.MESH)
    near = [peer(a, k) for a in range(3) for k in range(1, n)]
    near += [peer(a, k, b, k2) for a in range(3) for b in range(a) for k in range(1, n) for k2 in range(1, n)]
    for at in near:
        pl.semaphore_signal(
            barrier, inc=1, device_id=device(at, core), device_id_type=pl.DeviceIdType.MESH
        )
    pre_copy.start()
    rest_copy.start()

    here = coord + (core,)
    x_buf[(0,) + here] = q_ref[:, 0:LANES]
    x_buf[(1,) + here] = q_ref[:, LANES:PREFIX]
    row = row_ref[...]
    numbers = jnp.concatenate(
        [
            own_ref[...].astype(F32),
            lax.shift_right_logical(row, 6).astype(F32),
            (row & 63).astype(F32),
            jnp.zeros((QB, LANES - 3 * k_count), F32),
        ],
        axis=1,
    )
    x_buf[(2,) + here] = numbers.astype(BF16)
    for p in range(3):
        f_bufs[p][coord] = q_ref[:, col0[p] : col0[p + 1]]
    pl.semaphore_wait(barrier, 1 + len(near))

    def send(src, dst, ssem, rsem, target):
        pltpu.make_async_remote_copy(
            src_ref=src,
            dst_ref=dst,
            send_sem=ssem,
            recv_sem=rsem,
            device_id=target,
            device_id_type=pl.DeviceIdType.MESH,
        ).start()

    def wait_bytes(ref, sem):
        pltpu.make_async_copy(ref, ref, sem).wait()

    def phase_box(phase):
        if phase == 3:
            return (slice(None),) * 3
        return (slice(0, n - 1),) + (slice(None),) * phase + (0,) * (2 - phase)

    def gather_start(buf, tail, ssem, rsem, phase, p):
        if phase == 3:
            block = buf.at[(slice(None),) * 3 + tail]
            targets = [sibling]
        else:
            done = ORDERS[p][:phase]
            where = tuple(slice(None) if a in done else coord[a] for a in range(3))
            block = buf.at[where + tail]
            axis = ORDERS[p][phase]
            targets = [device(peer(axis, k), core) for k in far_first]
        for target in targets:
            send(block, block, ssem, rsem, target)

    def x_start(phase, p):
        gather_start(x_bufs[p], (core,), xs.at[phase], xr.at[p * 4 + phase], phase, p)

    def f_start(phase, p):
        gather_start(f_bufs[p], (), fs.at[p * 3 + phase], fr.at[p * 3 + phase], phase, p)

    def x_plane(p):
        block = x_bufs[p].at[here]
        first, second = ORDERS[p][:2]
        for k2 in range(n):
            for k in range(0 if k2 else 1, n):
                at = min(k2, 1)
                send(block, block, xs.at[at], xr.at[p * 4 + at], device(peer(first, k, second, k2), core))

    def x_wait(phase, p):
        wait_bytes(x_bufs[p].at[phase_box(phase) + (0,)], xr.at[p * 4 + phase])

    def x_step(phase):
        for p in range(3):
            if phase == 1:
                x_wait(0, p)
            x_wait(phase, p)
            if phase < 3:
                x_start(phase + 1, p)

    def f_step(phase):
        for p in range(3):
            wait_bytes(f_bufs[p].at[phase_box(phase)], fr.at[p * 3 + phase])
            if phase < 2:
                f_start(phase + 1, p)

    for p in range(3):
        x_plane(p)
    for p in range(3):
        f_start(0, p)
    x_step(1)
    f_step(0)
    x_step(2)
    f_step(1)

    def part_of(buf, t, *c):
        v = buf[(pl.ds(2 * t, 2), slice(None), slice(None)) + c]
        return v.astype(F32).reshape(chunk, v.shape[-1])

    def index(j, t, c):
        numbers = part_of(x_bufs[2], t, c)
        lane = lane_of(chunk)
        hit = (numbers == me_f) & (lane < k_count)
        high = pltpu.roll(numbers, LANES - k_count, 1)
        low = pltpu.roll(numbers, LANES - 2 * k_count, 1)
        any_hit = jnp.sum(jnp.where(hit, 1.0, 0.0), axis=1, keepdims=True)
        high = jnp.sum(jnp.where(hit, high, 0.0), axis=1, keepdims=True)
        low = jnp.sum(jnp.where(hit, low, 0.0), axis=1, keepdims=True)
        qi = lax.broadcasted_iota(jnp.int32, (chunk, chunk), 0)
        qj = lax.broadcasted_iota(jnp.int32, (chunk, chunk), 1)
        before = jnp.where(((qi >> 3) == (qj >> 3)) & (qj < qi), 1.0, 0.0).astype(BF16)
        rank = jnp.dot(
            before,
            jnp.broadcast_to(any_hit, (chunk, LANES)).astype(BF16),
            preferred_element_type=F32,
        )[:, 0:1]
        rank = jnp.where(any_hit > 0.0, rank, -1.0)
        q_of = lax.broadcasted_iota(jnp.int32, (chunk, n_slot), 0)
        s_of = lax.broadcasted_iota(jnp.int32, (chunk, n_slot), 1)
        sel = jnp.where(
            ((q_of >> 3) == (s_of >> 2)) & (rank == (s_of & 3).astype(F32)), 1.0, 0.0
        )
        sel_buf[j] = sel
        picked = jnp.dot(
            jnp.where(lane < 64, high, low).T.astype(BF16),
            sel.astype(BF16),
            preferred_element_type=F32,
        )
        row_of = (picked[0:1, :] * 64.0 + picked[64:65, :]).astype(jnp.int32)
        idx_v[pl.ds(j, 1), 0:n_slot] = row_of

    def half_of(j):
        return lax.rem(j, pairs), jnp.where(j < pairs, core, 1 - core)

    idx_copy = pltpu.make_async_copy(idx_v, idx_s, lsem.at[2])
    pre_copy.wait()

    factor = PREFIX ** (-0.5) * math.log2(math.e)
    tile = 512

    def prefix_of(j):
        t, c = half_of(j)
        return jnp.concatenate([part_of(x_bufs[0], t, c), part_of(x_bufs[1], t, c)], axis=1).astype(BF16)

    @pl.loop(0, 2)
    def _(h):
        @pl.when(h == 1)
        def _():
            x_step(3)

        @pl.loop(0, pairs)
        def _(t):
            j = h * pairs + t
            index(j, *half_of(j))

        @pl.when(h == 1)
        def _():
            idx_copy.start()
            send(sel_buf.at[pl.ds(pairs, pairs)], sel_got, ws.at[0], wr.at[0], sibling)

        @pl.loop(0, pairs)
        def _(t):
            j = h * pairs + t
            q = prefix_of(j)
            most = jnp.full((chunk, LANES), -jnp.inf, F32)
            for u in range(r_dev // tile):
                s = lax.dot_general(
                    q, pre_v[u * tile : (u + 1) * tile, :], NT, preferred_element_type=F32
                )
                logits[j, :, u * tile : (u + 1) * tile] = s
                for v in range(tile // LANES):
                    most = jnp.maximum(most, s[:, v * LANES : (v + 1) * LANES])
            tops[j] = jnp.broadcast_to(jnp.max(most, axis=1, keepdims=True) * factor, (chunk, LANES))

    idx_copy.wait()
    rest_copy.wait()

    half = pairs * n_slot // QB

    @pl.loop(0, 2)
    def _(h):
        @pl.loop(0, half)
        def _(gg):
            g = (1 - h) * half + gg
            sub = lax.broadcasted_iota(jnp.int32, (QB, width), 0)
            rows = jnp.zeros((QB, width), F32)
            for k in range(QB):
                at = g * QB + k
                i = jnp.clip(idx_s[lax.div(at, n_slot), lax.rem(at, n_slot)], 0, r_dev - 1)
                group = slab_v[i >> 3].astype(F32)
                rows = jnp.where(sub == k, pltpu.roll(group, (k - (i & 7)) & 7, 0), rows)
            rows_buf[g] = rows.astype(BF16)

        @pl.when(h == 0)
        def _():
            send(rows_buf.at[pl.ds(half, half)], rows_got, ws.at[1], wr.at[1], sibling)

    @pl.loop(0, n)
    def _(jj):
        j = lax.rem(jj + pairs, n)
        top = tops[j][:, 0:1]
        total = jnp.zeros((chunk, LANES), F32)
        acc = jnp.zeros((chunk, PREFIX), F32)
        for u in range(r_dev // tile):
            w = jnp.exp2(logits[j, :, u * tile : (u + 1) * tile] * factor - top)
            for v in range(tile // LANES):
                total = total + w[:, v * LANES : (v + 1) * LANES]
            acc = acc + jnp.dot(
                w.astype(BF16), pre_v[u * tile : (u + 1) * tile, :], preferred_element_type=F32
            )
        total = jnp.sum(total, axis=1, keepdims=True)
        lane = lane_of(chunk)
        p0, p1 = acc[:, :LANES], acc[:, LANES:]
        b = jnp.where(lane < 32, pltpu.roll(p0, 32, 1), pltpu.roll(p1, 32, 1))
        c = jnp.where(lane < F_LANE, pltpu.roll(p1, 64, 1), 0.0)
        c = jnp.where(lane == L_LANE, total, c)
        for p, v in enumerate((p0, b, c)):
            pay[j, p] = jnp.where(lane == M_LANE, top, v).reshape(box)

        @pl.when(jj < pairs)
        def _():
            send(pay.at[j], got0.at[jj], s0.at[jj], r0.at[jj], sibling)

    f_step(2)
    wait_bytes(sel_got, wr.at[0])
    wait_bytes(rows_got, wr.at[1])

    sibling_f = me_f + (1 - 2 * core).astype(F32)
    step = n_slot // QB

    @pl.loop(0, pairs)
    def _(t):
        def rows_of(lo, hi):
            groups = pl.ds(t * step, step)
            mine = rows_buf[groups, :, lo:hi].astype(F32).reshape(n_slot, hi - lo)
            other = rows_got[groups, :, lo:hi].astype(F32).reshape(n_slot, hi - lo)
            return jnp.concatenate([mine, other], axis=0).astype(BF16)

        scores = lax.dot_general(prefix_of(t), rows_of(0, PREFIX), NT, preferred_element_type=F32)
        for p in range(3):
            scores = scores + lax.dot_general(
                part_of(f_bufs[p], t).astype(BF16),
                rows_of(col0[p], col0[p + 1]),
                NT,
                preferred_element_type=F32,
            )
        lane = lane_of(chunk)
        numbers = jnp.where(lane < k_count, part_of(x_bufs[2], t, core), -1.0)
        full = jnp.sum(scores[:, :n_slot] * sel_buf[t], axis=1, keepdims=True)
        full2 = jnp.sum(scores[:, n_slot:] * sel_got[t], axis=1, keepdims=True)
        full = jnp.where(numbers == me_f, full, jnp.where(numbers == sibling_f, full2, 0.0))
        pay[t, 2] = pay[t, 2] + pltpu.roll(full, F_LANE, 1).reshape(box)

    def at_axis(axes, axis, index):
        return tuple(index if a == axis else slice(None) for a in axes)

    for p in range(3):

        @pl.loop(0, pairs)
        def _(t, p=p):
            if p == 0:
                wait_bytes(got0.at[t], r0.at[t])
            both = merge(p, [pay[t, p].reshape(chunk, LANES), got0[t, p].reshape(chunk, LANES)])
            mid0[p, pl.ds(2 * t, 2)] = both.reshape(box)

        axis = ORDERS[p][0]
        for k in far_first:
            to = peer(axis, k)
            send(mid0.at[(p,) + at_axis(range(3), axis, to[axis])], got1.at[p, k - 1], rs.at[0], rr.at[p], device(to, core))

    flat1 = (n * n * QB, LANES)
    for p in range(3):
        wait_bytes(got1.at[p], rr.at[p])
        first = ORDERS[p][0]
        own = mid0[(p,) + at_axis(range(3), first, coord[first])].reshape(flat1)
        blocks = [own] + [got1[p, k - 1].reshape(flat1) for k in range(1, n)]
        mid1[p] = merge(p, blocks).reshape(n, n, QB, LANES)
        left = [a for a in range(3) if a != first]
        for k in range(n * n - 1):
            k2, k3 = (k + 1) // n, (k + 1) % n
            to = peer(left[0], k2, left[1], k3)
            send(mid1.at[p, to[left[0]], to[left[1]]], got2.at[p, k], rs.at[1], rr.at[3 + p], device(to, core))

    out = []
    for p in range(3):
        wait_bytes(got2.at[p], rr.at[3 + p])
        left = [coord[a] for a in range(3) if a != ORDERS[p][0]]
        own = mid1[p, left[0], left[1]]
        out.append(merge(p, [own] + [got2[p, k] for k in range(n * n - 1)]))

    lane = lane_of(QB)
    a, b, c = out
    total = c[:, L_LANE : L_LANE + 1]
    b_back = pltpu.roll(b, 96, 1)
    out_ref[:, 0:LANES] = jnp.where(lane < 96, a, b_back) / total
    out_ref[:, LANES:PREFIX] = jnp.where(lane < 64, b_back, pltpu.roll(c, 64, 1)) / total
    lse = c[:, M_LANE:] * math.log(2.0) + jnp.log(total)
    full = pltpu.roll(c, LANES - F_LANE, 1) * width ** (-0.5)
    out_ref[:, PREFIX : PREFIX + LANES] = full - lse
    out_ref[:, PREFIX + LANES :] = jnp.broadcast_to(lse, (QB, LANES))

    for phase in range(4):
        wait_bytes(x_buf.at[(slice(None),) + phase_box(phase) + (0,)], xs.at[phase])
    for phase in range(3):
        for p in range(3):
            wait_bytes(f_bufs[p].at[phase_box(phase)], fs.at[p * 3 + phase])
    wait_bytes(sel_got, ws.at[0])
    wait_bytes(rows_got, ws.at[1])
    for t in range(pairs):
        wait_bytes(got0.at[t], s0.at[t])
    wait_bytes(got1, rs.at[0])
    wait_bytes(got2, rs.at[1])


def split(in_ref, pooled_ref, lse_ref, margin_ref):
    pooled_ref[...] = in_ref[:, 0:PREFIX]
    margin_ref[...] = in_ref[:, PREFIX : PREFIX + margin_ref.shape[1]]
    here = lax.broadcasted_iota(jnp.int32, (QB, LANES), 0) == lane_of(QB)
    lse = jnp.sum(jnp.where(here, in_ref[:, PREFIX + LANES :], 0.0), axis=0, keepdims=True)
    lse_ref[...] = lse[:, 0:QB]


def make(mesh, dims):
    def on_device(queries, slab, cand_owner, cand_row):
        width = queries.shape[1]
        r_dev = slab.shape[0]
        k_count = cand_owner.shape[1]
        tiles = (width - PREFIX) // LANES
        n0 = -(-tiles // 3)
        n1 = -(-(tiles - n0) // 2)
        col0 = (PREFIX, PREFIX + n0 * LANES, PREFIX + (n0 + n1) * LANES, width)
        n = dims[0]
        chunk = 2 * n * n * QB
        n_slot = chunk // QB * SLOTS
        vmem = pltpu.VMEM
        dma = pltpu.SemaphoreType.DMA
        spec = pl.BlockSpec(memory_space=pltpu.VMEM)
        merged = pl.pallas_call(
            functools.partial(kernel, dims, col0),
            out_shape=jax.ShapeDtypeStruct((QB, PREFIX + 2 * LANES), F32),
            in_specs=[spec, pl.BlockSpec(memory_space=pl.ANY), pl.BlockSpec(memory_space=pl.ANY), spec, spec],
            out_specs=spec,
            scratch_shapes=[
                vmem((r_dev, PREFIX), BF16),
                vmem((r_dev // QB, QB, width), BF16),
                vmem((3, n, n, n, 2, QB, LANES), BF16),
                vmem((n, n, n, QB, col0[1] - col0[0]), BF16),
                vmem((n, n, n, QB, col0[2] - col0[1]), BF16),
                vmem((n, n, n, QB, col0[3] - col0[2]), BF16),
                vmem((n, chunk, n_slot), F32),
                vmem((n // 2, chunk, n_slot), F32),
                vmem((QB, LANES), jnp.int32),
                pltpu.SMEM((QB, LANES), jnp.int32),
                vmem((n * n_slot // QB, QB, width), BF16),
                vmem((n * n_slot // QB // 2, QB, width), BF16),
                vmem((n, chunk, r_dev), F32),
                vmem((n, chunk, LANES), F32),
                vmem((n, 3) + (2, n, n, QB, LANES), F32),
                vmem((n // 2, 3) + (2, n, n, QB, LANES), F32),
                vmem((3, n, n, n, QB, LANES), F32),
                vmem((3, n - 1, n, n, QB, LANES), F32),
                vmem((3, n, n, QB, LANES), F32),
                vmem((3, n * n - 1, QB, LANES), F32),
                dma((3,)),
                dma((4,)),
                dma((12,)),
                dma((9,)),
                dma((9,)),
                dma((2,)),
                dma((2,)),
                dma((n // 2,)),
                dma((n // 2,)),
                dma((2,)),
                dma((6,)),
            ],
            compiler_params=pltpu.CompilerParams(
                collective_id=0, has_side_effects=True, vmem_limit_bytes=56 * 2**20
            ),
        )(queries, slab, slab.reshape(r_dev // QB, QB, width), cand_owner, cand_row)
        pooled, lse, margin = pl.pallas_call(
            split,
            out_shape=(
                jax.ShapeDtypeStruct((QB, PREFIX), F32),
                jax.ShapeDtypeStruct((1, QB), F32),
                jax.ShapeDtypeStruct((QB, k_count), F32),
            ),
            in_specs=[spec],
            out_specs=(spec, spec, spec),
        )(merged)
        return pooled, lse.reshape(QB), margin

    both = ("index", "query")
    return jax.shard_map(
        on_device,
        mesh=mesh,
        in_specs=(P(both, None),) * 4,
        out_specs=(P(both, None), P(both), P(both, None)),
        check_vma=False,
    )


def solution(mesh):
    side = math.isqrt(mesh.shape["index"])
    return make(mesh, (side, side, mesh.shape["query"] // 2))
```

```python
import functools
import math

import jax
import jax.numpy as jnp
from jax import lax
from jax.experimental import pallas as pl
from jax.experimental.pallas import tpu as pltpu
from jax.sharding import PartitionSpec as P

PREFIX = 256
LANES = 128
QB = 8
SLOTS = 4
F32 = jnp.float32
BF16 = jnp.bfloat16
ORDERS = ((1, 0, 2), (0, 2, 1), (2, 1, 0))
NT = (((1,), (1,)), ((), ()))
M_LANE = 127
L_LANE = 96
F_LANE = 64


def lane_of(rows):
    return lax.broadcasted_iota(jnp.int32, (rows, LANES), 1)


def merge(part, blocks):
    lane = lane_of(blocks[0].shape[0])
    maxima = [b[:, M_LANE:] for b in blocks]
    top = functools.reduce(jnp.maximum, maxima)
    total = None
    for b, m in zip(blocks, maxima):
        s = jnp.broadcast_to(jnp.exp2(m - top), b.shape)
        if part == 2:
            s = jnp.where((lane >= F_LANE) & (lane < L_LANE), 1.0, s)
        total = b * s if total is None else total + b * s
    return jnp.where(lane == M_LANE, top, total)


def kernel(
    dims,
    col0,
    q_ref,
    slab_ref,
    groups_ref,
    own_ref,
    row_ref,
    out_ref,
    pre_v,
    slab_v,
    x_buf,
    f0,
    f1,
    f2,
    sel_buf,
    sel_got,
    idx_v,
    idx_s,
    rows_buf,
    rows_got,
    logits,
    tops,
    pay,
    got0,
    mid0,
    got1,
    mid1,
    got2,
    lsem,
    xs,
    xr,
    fs,
    fr,
    ws,
    wr,
    s0,
    r0,
    rs,
    rr,
):
    width = q_ref.shape[1]
    r_dev = slab_ref.shape[0]
    ii, qq = lax.axis_index("index"), lax.axis_index("query")
    coord = (lax.div(ii, dims[1]), lax.rem(ii, dims[1]), lax.div(qq, 2))
    core = lax.rem(qq, 2)
    me_f = (ii * (dims[2] * 2) + qq).astype(F32)
    n = dims[0]
    pairs = n // 2
    k_count = row_ref.shape[1]
    box = (2, n, n, QB, LANES)
    chunk = 2 * n * n * QB
    n_slot = chunk // QB * SLOTS
    f_bufs = (f0, f1, f2)
    x_bufs = [x_buf.at[p] for p in range(3)]

    def device(at, c):
        return (at[0] * n + at[1], at[2] * 2 + c)

    moved = [[coord[a]] + [lax.rem(coord[a] + k, n) for k in range(1, n)] for a in range(3)]

    def peer(axis, k, axis2=None, k2=0):
        at = list(coord)
        at[axis] = moved[axis][k]
        if axis2 is not None:
            at[axis2] = moved[axis2][k2]
        return tuple(at)

    sibling = device(coord, 1 - core)
    far_first = sorted(range(1, n), key=lambda k: -min(k, n - k))

    pre_copy = pltpu.make_async_copy(slab_ref.at[:, pl.ds(0, PREFIX)], pre_v, lsem.at[0])
    rest_copy = pltpu.make_async_copy(groups_ref, slab_v, lsem.at[1])

    barrier = pltpu.get_barrier_semaphore()
    pl.semaphore_signal(barrier, inc=1, device_id=sibling, device_id_type=pl.DeviceIdType.MESH)
    near = [peer(a, k) for a in range(3) for k in range(1, n)]
    near += [peer(a, k, b, k2) for a in range(3) for b in range(a) for k in range(1, n) for k2 in range(1, n)]
    for at in near:
        pl.semaphore_signal(
            barrier, inc=1, device_id=device(at, core), device_id_type=pl.DeviceIdType.MESH
        )
    pre_copy.start()
    rest_copy.start()

    here = coord + (core,)
    x_buf[(0,) + here] = q_ref[:, 0:LANES]
    x_buf[(1,) + here] = q_ref[:, LANES:PREFIX]
    row = row_ref[...]
    numbers = jnp.concatenate(
        [
            own_ref[...].astype(F32),
            lax.shift_right_logical(row, 6).astype(F32),
            (row & 63).astype(F32),
            jnp.zeros((QB, LANES - 3 * k_count), F32),
        ],
        axis=1,
    )
    x_buf[(2,) + here] = numbers.astype(BF16)
    for p in range(3):
        f_bufs[p][coord] = q_ref[:, col0[p] : col0[p + 1]]
    pl.semaphore_wait(barrier, 1 + len(near))

    def send(src, dst, ssem, rsem, target):
        pltpu.make_async_remote_copy(
            src_ref=src,
            dst_ref=dst,
            send_sem=ssem,
            recv_sem=rsem,
            device_id=target,
            device_id_type=pl.DeviceIdType.MESH,
        ).start()

    def wait_bytes(ref, sem):
        pltpu.make_async_copy(ref, ref, sem).wait()

    def phase_box(phase):
        if phase == 3:
            return (slice(None),) * 3
        return (slice(0, n - 1),) + (slice(None),) * phase + (0,) * (2 - phase)

    def gather_start(buf, tail, ssem, rsem, phase, p):
        if phase == 3:
            block = buf.at[(slice(None),) * 3 + tail]
            targets = [sibling]
        else:
            done = ORDERS[p][:phase]
            where = tuple(slice(None) if a in done else coord[a] for a in range(3))
            block = buf.at[where + tail]
            axis = ORDERS[p][phase]
            targets = [device(peer(axis, k), core) for k in far_first]
        for target in targets:
            send(block, block, ssem, rsem, target)

    def x_start(phase, p):
        gather_start(x_bufs[p], (core,), xs.at[phase], xr.at[p * 4 + phase], phase, p)

    def f_start(phase, p):
        gather_start(f_bufs[p], (), fs.at[p * 3 + phase], fr.at[p * 3 + phase], phase, p)

    def x_plane(p):
        block = x_bufs[p].at[here]
        first, second = ORDERS[p][:2]
        for k2 in range(n):
            for k in range(0 if k2 else 1, n):
                at = min(k2, 1)
                send(block, block, xs.at[at], xr.at[p * 4 + at], device(peer(first, k, second, k2), core))

    def x_wait(phase, p):
        wait_bytes(x_bufs[p].at[phase_box(phase) + (0,)], xr.at[p * 4 + phase])

    def x_step(phase):
        for p in range(3):
            if phase == 1:
                x_wait(0, p)
            x_wait(phase, p)
            if phase < 3:
                x_start(phase + 1, p)

    def f_step(phase):
        for p in range(3):
            wait_bytes(f_bufs[p].at[phase_box(phase)], fr.at[p * 3 + phase])
            if phase < 2:
                f_start(phase + 1, p)

    for p in range(3):
        x_plane(p)
    for p in range(3):
        f_start(0, p)
    x_step(1)
    f_step(0)
    x_step(2)
    f_step(1)

    def part_of(buf, t, *c):
        v = buf[(pl.ds(2 * t, 2), slice(None), slice(None)) + c]
        return v.astype(F32).reshape(chunk, v.shape[-1])

    def index(j, t, c):
        numbers = part_of(x_bufs[2], t, c)
        lane = lane_of(chunk)
        hit = (numbers == me_f) & (lane < k_count)
        high = pltpu.roll(numbers, LANES - k_count, 1)
        low = pltpu.roll(numbers, LANES - 2 * k_count, 1)
        any_hit = jnp.sum(jnp.where(hit, 1.0, 0.0), axis=1, keepdims=True)
        high = jnp.sum(jnp.where(hit, high, 0.0), axis=1, keepdims=True)
        low = jnp.sum(jnp.where(hit, low, 0.0), axis=1, keepdims=True)
        qi = lax.broadcasted_iota(jnp.int32, (chunk, chunk), 0)
        qj = lax.broadcasted_iota(jnp.int32, (chunk, chunk), 1)
        before = jnp.where(((qi >> 3) == (qj >> 3)) & (qj < qi), 1.0, 0.0).astype(BF16)
        rank = jnp.dot(
            before,
            jnp.broadcast_to(any_hit, (chunk, LANES)).astype(BF16),
            preferred_element_type=F32,
        )[:, 0:1]
        rank = jnp.where(any_hit > 0.0, rank, -1.0)
        q_of = lax.broadcasted_iota(jnp.int32, (chunk, n_slot), 0)
        s_of = lax.broadcasted_iota(jnp.int32, (chunk, n_slot), 1)
        sel = jnp.where(
            ((q_of >> 3) == (s_of >> 2)) & (rank == (s_of & 3).astype(F32)), 1.0, 0.0
        )
        sel_buf[j] = sel
        picked = jnp.dot(
            jnp.where(lane < 64, high, low).T.astype(BF16),
            sel.astype(BF16),
            preferred_element_type=F32,
        )
        row_of = (picked[0:1, :] * 64.0 + picked[64:65, :]).astype(jnp.int32)
        idx_v[pl.ds(j, 1), 0:n_slot] = row_of

    def half_of(j):
        return lax.rem(j, pairs), jnp.where(j < pairs, core, 1 - core)

    idx_copy = pltpu.make_async_copy(idx_v, idx_s, lsem.at[2])
    pre_copy.wait()

    factor = PREFIX ** (-0.5) * math.log2(math.e)
    tile = 512
    side = pairs * chunk

    def prefix_of(j):
        t, c = half_of(j)
        return jnp.concatenate([part_of(x_bufs[0], t, c), part_of(x_bufs[1], t, c)], axis=1).astype(BF16)

    @pl.loop(0, 2)
    def _(h):
        @pl.when(h == 1)
        def _():
            x_step(3)

        @pl.loop(0, pairs)
        def _(t):
            j = h * pairs + t
            index(j, *half_of(j))

        @pl.when(h == 1)
        def _():
            idx_copy.start()
            send(sel_buf.at[pl.ds(pairs, pairs)], sel_got, ws.at[0], wr.at[0], sibling)

        q = jnp.concatenate([prefix_of(h * pairs + t) for t in range(pairs)], axis=0)
        most = jnp.full((side, LANES), -jnp.inf, F32)
        for u in range(r_dev // tile):
            s = lax.dot_general(
                q, pre_v[u * tile : (u + 1) * tile, :], NT, preferred_element_type=F32
            )
            logits[h, :, u * tile : (u + 1) * tile] = s
            for v in range(tile // LANES):
                most = jnp.maximum(most, s[:, v * LANES : (v + 1) * LANES])
        tops[h] = jnp.broadcast_to(jnp.max(most, axis=1, keepdims=True) * factor, (side, LANES))

    idx_copy.wait()
    rest_copy.wait()

    half = pairs * n_slot // QB

    @pl.loop(0, 2)
    def _(h):
        @pl.loop(0, half, unroll=4)
        def _(gg):
            g = (1 - h) * half + gg
            sub = lax.broadcasted_iota(jnp.int32, (QB, width), 0)
            rows = jnp.zeros((QB, width), F32)
            for k in range(QB):
                at = g * QB + k
                i = jnp.clip(idx_s[lax.div(at, n_slot), lax.rem(at, n_slot)], 0, r_dev - 1)
                group = slab_v[i >> 3].astype(F32)
                rows = jnp.where(sub == k, pltpu.roll(group, (k - (i & 7)) & 7, 0), rows)
            rows_buf[g] = rows.astype(BF16)

        @pl.when(h == 0)
        def _():
            send(rows_buf.at[pl.ds(half, half)], rows_got, ws.at[1], wr.at[1], sibling)

    @pl.loop(0, 2)
    def _(hh):
        h = 1 - hh
        top = tops[h][:, 0:1]
        total = jnp.zeros((side, LANES), F32)
        acc = jnp.zeros((side, PREFIX), F32)
        for u in range(r_dev // tile):
            w = jnp.exp2(logits[h, :, u * tile : (u + 1) * tile] * factor - top)
            for v in range(tile // LANES):
                total = total + w[:, v * LANES : (v + 1) * LANES]
            acc = acc + jnp.dot(
                w.astype(BF16), pre_v[u * tile : (u + 1) * tile, :], preferred_element_type=F32
            )
        total = jnp.sum(total, axis=1, keepdims=True)
        lane = lane_of(side)
        p0, p1 = acc[:, :LANES], acc[:, LANES:]
        b = jnp.where(lane < 32, pltpu.roll(p0, 32, 1), pltpu.roll(p1, 32, 1))
        c = jnp.where(lane < F_LANE, pltpu.roll(p1, 64, 1), 0.0)
        c = jnp.where(lane == L_LANE, total, c)
        for p, v in enumerate((p0, b, c)):
            pay[pl.ds(h * pairs, pairs), p] = jnp.where(lane == M_LANE, top, v).reshape((pairs,) + box)

        @pl.when(hh == 0)
        def _():
            for t in range(pairs):
                send(pay.at[pairs + t], got0.at[t], s0.at[t], r0.at[t], sibling)

    f_step(2)
    wait_bytes(sel_got, wr.at[0])
    wait_bytes(rows_got, wr.at[1])

    sibling_f = me_f + (1 - 2 * core).astype(F32)
    step = n_slot // QB

    @pl.loop(0, pairs)
    def _(t):
        def rows_of(lo, hi):
            groups = pl.ds(t * step, step)
            mine = rows_buf[groups, :, lo:hi].astype(F32).reshape(n_slot, hi - lo)
            other = rows_got[groups, :, lo:hi].astype(F32).reshape(n_slot, hi - lo)
            return jnp.concatenate([mine, other], axis=0).astype(BF16)

        scores = lax.dot_general(prefix_of(t), rows_of(0, PREFIX), NT, preferred_element_type=F32)
        for p in range(3):
            scores = scores + lax.dot_general(
                part_of(f_bufs[p], t).astype(BF16),
                rows_of(col0[p], col0[p + 1]),
                NT,
                preferred_element_type=F32,
            )
        lane = lane_of(chunk)
        numbers = jnp.where(lane < k_count, part_of(x_bufs[2], t, core), -1.0)
        full = jnp.sum(scores[:, :n_slot] * sel_buf[t], axis=1, keepdims=True)
        full2 = jnp.sum(scores[:, n_slot:] * sel_got[t], axis=1, keepdims=True)
        full = jnp.where(numbers == me_f, full, jnp.where(numbers == sibling_f, full2, 0.0))
        pay[t, 2] = pay[t, 2] + pltpu.roll(full, F_LANE, 1).reshape(box)

    def at_axis(axes, axis, index):
        return tuple(index if a == axis else slice(None) for a in axes)

    for p in range(3):

        @pl.loop(0, pairs)
        def _(t, p=p):
            if p == 0:
                wait_bytes(got0.at[t], r0.at[t])
            both = merge(p, [pay[t, p].reshape(chunk, LANES), got0[t, p].reshape(chunk, LANES)])
            mid0[p, pl.ds(2 * t, 2)] = both.reshape(box)

        axis = ORDERS[p][0]
        for k in far_first:
            to = peer(axis, k)
            send(mid0.at[(p,) + at_axis(range(3), axis, to[axis])], got1.at[p, k - 1], rs.at[0], rr.at[p], device(to, core))

    flat1 = (n * n * QB, LANES)
    for p in range(3):
        wait_bytes(got1.at[p], rr.at[p])
        first = ORDERS[p][0]
        own = mid0[(p,) + at_axis(range(3), first, coord[first])].reshape(flat1)
        blocks = [own] + [got1[p, k - 1].reshape(flat1) for k in range(1, n)]
        mid1[p] = merge(p, blocks).reshape(n, n, QB, LANES)
        left = [a for a in range(3) if a != first]
        for k in range(n * n - 1):
            k2, k3 = (k + 1) // n, (k + 1) % n
            to = peer(left[0], k2, left[1], k3)
            send(mid1.at[p, to[left[0]], to[left[1]]], got2.at[p, k], rs.at[1], rr.at[3 + p], device(to, core))

    out = []
    for p in range(3):
        wait_bytes(got2.at[p], rr.at[3 + p])
        left = [coord[a] for a in range(3) if a != ORDERS[p][0]]
        own = mid1[p, left[0], left[1]]
        out.append(merge(p, [own] + [got2[p, k] for k in range(n * n - 1)]))

    lane = lane_of(QB)
    a, b, c = out
    total = c[:, L_LANE : L_LANE + 1]
    b_back = pltpu.roll(b, 96, 1)
    out_ref[:, 0:LANES] = jnp.where(lane < 96, a, b_back) / total
    out_ref[:, LANES:PREFIX] = jnp.where(lane < 64, b_back, pltpu.roll(c, 64, 1)) / total
    lse = c[:, M_LANE:] * math.log(2.0) + jnp.log(total)
    full = pltpu.roll(c, LANES - F_LANE, 1) * width ** (-0.5)
    out_ref[:, PREFIX : PREFIX + LANES] = full - lse
    out_ref[:, PREFIX + LANES :] = jnp.broadcast_to(lse, (QB, LANES))

    for phase in range(4):
        wait_bytes(x_buf.at[(slice(None),) + phase_box(phase) + (0,)], xs.at[phase])
    for phase in range(3):
        for p in range(3):
            wait_bytes(f_bufs[p].at[phase_box(phase)], fs.at[p * 3 + phase])
    wait_bytes(sel_got, ws.at[0])
    wait_bytes(rows_got, ws.at[1])
    for t in range(pairs):
        wait_bytes(got0.at[t], s0.at[t])
    wait_bytes(got1, rs.at[0])
    wait_bytes(got2, rs.at[1])


def split(in_ref, pooled_ref, lse_ref, margin_ref):
    pooled_ref[...] = in_ref[:, 0:PREFIX]
    margin_ref[...] = in_ref[:, PREFIX : PREFIX + margin_ref.shape[1]]
    here = lax.broadcasted_iota(jnp.int32, (QB, LANES), 0) == lane_of(QB)
    lse = jnp.sum(jnp.where(here, in_ref[:, PREFIX + LANES :], 0.0), axis=0, keepdims=True)
    lse_ref[...] = lse[:, 0:QB]


def make(mesh, dims):
    def on_device(queries, slab, cand_owner, cand_row):
        width = queries.shape[1]
        r_dev = slab.shape[0]
        k_count = cand_owner.shape[1]
        tiles = (width - PREFIX) // LANES
        n0 = -(-tiles // 3)
        n1 = -(-(tiles - n0) // 2)
        col0 = (PREFIX, PREFIX + n0 * LANES, PREFIX + (n0 + n1) * LANES, width)
        n = dims[0]
        chunk = 2 * n * n * QB
        n_slot = chunk // QB * SLOTS
        vmem = pltpu.VMEM
        dma = pltpu.SemaphoreType.DMA
        spec = pl.BlockSpec(memory_space=pltpu.VMEM)
        merged = pl.pallas_call(
            functools.partial(kernel, dims, col0),
            out_shape=jax.ShapeDtypeStruct((QB, PREFIX + 2 * LANES), F32),
            in_specs=[spec, pl.BlockSpec(memory_space=pl.ANY), pl.BlockSpec(memory_space=pl.ANY), spec, spec],
            out_specs=spec,
            scratch_shapes=[
                vmem((r_dev, PREFIX), BF16),
                vmem((r_dev // QB, QB, width), BF16),
                vmem((3, n, n, n, 2, QB, LANES), BF16),
                vmem((n, n, n, QB, col0[1] - col0[0]), BF16),
                vmem((n, n, n, QB, col0[2] - col0[1]), BF16),
                vmem((n, n, n, QB, col0[3] - col0[2]), BF16),
                vmem((n, chunk, n_slot), F32),
                vmem((n // 2, chunk, n_slot), F32),
                vmem((QB, LANES), jnp.int32),
                pltpu.SMEM((QB, LANES), jnp.int32),
                vmem((n * n_slot // QB, QB, width), BF16),
                vmem((n * n_slot // QB // 2, QB, width), BF16),
                vmem((2, n // 2 * chunk, r_dev), F32),
                vmem((2, n // 2 * chunk, LANES), F32),
                vmem((n, 3) + (2, n, n, QB, LANES), F32),
                vmem((n // 2, 3) + (2, n, n, QB, LANES), F32),
                vmem((3, n, n, n, QB, LANES), F32),
                vmem((3, n - 1, n, n, QB, LANES), F32),
                vmem((3, n, n, QB, LANES), F32),
                vmem((3, n * n - 1, QB, LANES), F32),
                dma((3,)),
                dma((4,)),
                dma((12,)),
                dma((9,)),
                dma((9,)),
                dma((2,)),
                dma((2,)),
                dma((n // 2,)),
                dma((n // 2,)),
                dma((2,)),
                dma((6,)),
            ],
            compiler_params=pltpu.CompilerParams(
                collective_id=0, has_side_effects=True, vmem_limit_bytes=56 * 2**20
            ),
        )(queries, slab, slab.reshape(r_dev // QB, QB, width), cand_owner, cand_row)
        pooled, lse, margin = pl.pallas_call(
            split,
            out_shape=(
                jax.ShapeDtypeStruct((QB, PREFIX), F32),
                jax.ShapeDtypeStruct((1, QB), F32),
                jax.ShapeDtypeStruct((QB, k_count), F32),
            ),
            in_specs=[spec],
            out_specs=(spec, spec, spec),
        )(merged)
        return pooled, lse.reshape(QB), margin

    both = ("index", "query")
    return jax.shard_map(
        on_device,
        mesh=mesh,
        in_specs=(P(both, None),) * 4,
        out_specs=(P(both, None), P(both), P(both, None)),
        check_vma=False,
    )


def solution(mesh):
    side = math.isqrt(mesh.shape["index"])
    return make(mesh, (side, side, mesh.shape["query"] // 2))
```

```python
import functools
import math

import jax
import jax.numpy as jnp
from jax import lax
from jax.experimental import pallas as pl
from jax.experimental.pallas import tpu as pltpu
from jax.sharding import PartitionSpec as P

PREFIX = 256
LANES = 128
QB = 8
SLOTS = 4
F32 = jnp.float32
BF16 = jnp.bfloat16
ORDERS = ((1, 0, 2), (0, 2, 1), (2, 1, 0))
NT = (((1,), (1,)), ((), ()))
M_LANE = 127
L_LANE = 96
F_LANE = 64


def lane_of(rows):
    return lax.broadcasted_iota(jnp.int32, (rows, LANES), 1)


def merge(part, blocks):
    lane = lane_of(blocks[0].shape[0])
    maxima = [b[:, M_LANE:] for b in blocks]
    top = functools.reduce(jnp.maximum, maxima)
    total = None
    for b, m in zip(blocks, maxima):
        s = jnp.broadcast_to(jnp.exp2(m - top), b.shape)
        if part == 2:
            s = jnp.where((lane >= F_LANE) & (lane < L_LANE), 1.0, s)
        total = b * s if total is None else total + b * s
    return jnp.where(lane == M_LANE, top, total)


def kernel(
    dims,
    col0,
    q_ref,
    slab_ref,
    groups_ref,
    own_ref,
    row_ref,
    out_ref,
    pre_v,
    slab_v,
    x_buf,
    f0,
    f1,
    f2,
    sel_buf,
    sel_got,
    idx_v,
    idx_s,
    rows_buf,
    rows_got,
    logits,
    tops,
    pay,
    got0,
    mid0,
    got1,
    mid1,
    got2,
    lsem,
    xs,
    xr,
    fs,
    fr,
    ws,
    wr,
    s0,
    r0,
    rs,
    rr,
):
    width = q_ref.shape[1]
    r_dev = slab_ref.shape[0]
    ii, qq = lax.axis_index("index"), lax.axis_index("query")
    coord = (lax.div(ii, dims[1]), lax.rem(ii, dims[1]), lax.div(qq, 2))
    core = lax.rem(qq, 2)
    me_f = (ii * (dims[2] * 2) + qq).astype(F32)
    n = dims[0]
    pairs = n // 2
    k_count = row_ref.shape[1]
    box = (2, n, n, QB, LANES)
    chunk = 2 * n * n * QB
    n_slot = chunk // QB * SLOTS
    f_bufs = (f0, f1, f2)
    x_bufs = [x_buf.at[p] for p in range(3)]

    def device(at, c):
        return (at[0] * n + at[1], at[2] * 2 + c)

    moved = [[coord[a]] + [lax.rem(coord[a] + k, n) for k in range(1, n)] for a in range(3)]

    def peer(axis, k, axis2=None, k2=0):
        at = list(coord)
        at[axis] = moved[axis][k]
        if axis2 is not None:
            at[axis2] = moved[axis2][k2]
        return tuple(at)

    sibling = device(coord, 1 - core)
    far_first = sorted(range(1, n), key=lambda k: -min(k, n - k))

    pre_copy = pltpu.make_async_copy(slab_ref.at[:, pl.ds(0, PREFIX)], pre_v, lsem.at[0])
    rest_copy = pltpu.make_async_copy(groups_ref, slab_v, lsem.at[1])

    barrier = pltpu.get_barrier_semaphore()
    pl.semaphore_signal(barrier, inc=1, device_id=sibling, device_id_type=pl.DeviceIdType.MESH)
    near = [peer(a, k) for a in range(3) for k in range(1, n)]
    near += [peer(a, k, b, k2) for a in range(3) for b in range(a) for k in range(1, n) for k2 in range(1, n)]
    for at in near:
        pl.semaphore_signal(
            barrier, inc=1, device_id=device(at, core), device_id_type=pl.DeviceIdType.MESH
        )
    pre_copy.start()
    rest_copy.start()

    here = coord + (core,)
    x_buf[(0,) + here] = q_ref[:, 0:LANES]
    x_buf[(1,) + here] = q_ref[:, LANES:PREFIX]
    row = row_ref[...]
    numbers = jnp.concatenate(
        [
            own_ref[...].astype(F32),
            lax.shift_right_logical(row, 6).astype(F32),
            (row & 63).astype(F32),
            jnp.zeros((QB, LANES - 3 * k_count), F32),
        ],
        axis=1,
    )
    x_buf[(2,) + here] = numbers.astype(BF16)
    for p in range(3):
        f_bufs[p][coord] = q_ref[:, col0[p] : col0[p + 1]]
    pl.semaphore_wait(barrier, 1 + len(near))

    def send(src, dst, ssem, rsem, target):
        pltpu.make_async_remote_copy(
            src_ref=src,
            dst_ref=dst,
            send_sem=ssem,
            recv_sem=rsem,
            device_id=target,
            device_id_type=pl.DeviceIdType.MESH,
        ).start()

    def wait_bytes(ref, sem):
        pltpu.make_async_copy(ref, ref, sem).wait()

    def phase_box(phase):
        if phase == 3:
            return (slice(None),) * 3
        return (slice(0, n - 1),) + (slice(None),) * phase + (0,) * (2 - phase)

    def gather_start(buf, tail, ssem, rsem, phase, p):
        if phase == 3:
            block = buf.at[(slice(None),) * 3 + tail]
            targets = [sibling]
        else:
            done = ORDERS[p][:phase]
            where = tuple(slice(None) if a in done else coord[a] for a in range(3))
            block = buf.at[where + tail]
            axis = ORDERS[p][phase]
            targets = [device(peer(axis, k), core) for k in far_first]
        for target in targets:
            send(block, block, ssem, rsem, target)

    def x_start(phase, p):
        gather_start(x_bufs[p], (core,), xs.at[phase], xr.at[p * 4 + phase], phase, p)

    def f_start(phase, p):
        gather_start(f_bufs[p], (), fs.at[p * 3 + phase], fr.at[p * 3 + phase], phase, p)

    def x_plane(p):
        block = x_bufs[p].at[here]
        first, second = ORDERS[p][:2]
        for k2 in range(n):
            for k in range(0 if k2 else 1, n):
                at = min(k2, 1)
                send(block, block, xs.at[at], xr.at[p * 4 + at], device(peer(first, k, second, k2), core))

    def x_wait(phase, p):
        wait_bytes(x_bufs[p].at[phase_box(phase) + (0,)], xr.at[p * 4 + phase])

    def x_step(phase):
        for p in range(3):
            if phase == 1:
                x_wait(0, p)
            x_wait(phase, p)
            if phase < 3:
                x_start(phase + 1, p)

    def f_step(phase):
        for p in range(3):
            wait_bytes(f_bufs[p].at[phase_box(phase)], fr.at[p * 3 + phase])
            if phase < 2:
                f_start(phase + 1, p)

    for p in range(3):
        x_plane(p)
    for p in range(3):
        f_start(0, p)
    x_step(1)
    f_step(0)
    x_step(2)
    f_step(1)

    def part_of(buf, t, *c):
        v = buf[(pl.ds(2 * t, 2), slice(None), slice(None)) + c]
        return v.astype(F32).reshape(chunk, v.shape[-1])

    def index(j, t, c):
        numbers = part_of(x_bufs[2], t, c)
        lane = lane_of(chunk)
        hit = (numbers == me_f) & (lane < k_count)
        high = pltpu.roll(numbers, LANES - k_count, 1)
        low = pltpu.roll(numbers, LANES - 2 * k_count, 1)
        any_hit = jnp.sum(jnp.where(hit, 1.0, 0.0), axis=1, keepdims=True)
        high = jnp.sum(jnp.where(hit, high, 0.0), axis=1, keepdims=True)
        low = jnp.sum(jnp.where(hit, low, 0.0), axis=1, keepdims=True)
        qi = lax.broadcasted_iota(jnp.int32, (chunk, chunk), 0)
        qj = lax.broadcasted_iota(jnp.int32, (chunk, chunk), 1)
        before = jnp.where(((qi >> 3) == (qj >> 3)) & (qj < qi), 1.0, 0.0).astype(BF16)
        rank = jnp.dot(
            before,
            jnp.broadcast_to(any_hit, (chunk, LANES)).astype(BF16),
            preferred_element_type=F32,
        )[:, 0:1]
        rank = jnp.where(any_hit > 0.0, rank, -1.0)
        q_of = lax.broadcasted_iota(jnp.int32, (chunk, n_slot), 0)
        s_of = lax.broadcasted_iota(jnp.int32, (chunk, n_slot), 1)
        sel = jnp.where(
            ((q_of >> 3) == (s_of >> 2)) & (rank == (s_of & 3).astype(F32)), 1.0, 0.0
        )
        sel_buf[j] = sel
        picked = jnp.dot(
            jnp.where(lane < 64, high, low).T.astype(BF16),
            sel.astype(BF16),
            preferred_element_type=F32,
        )
        row_of = (picked[0:1, :] * 64.0 + picked[64:65, :]).astype(jnp.int32)
        idx_v[pl.ds(j, 1), 0:n_slot] = row_of

    def half_of(j):
        return lax.rem(j, pairs), jnp.where(j < pairs, core, 1 - core)

    idx_copy = pltpu.make_async_copy(idx_v, idx_s, lsem.at[2])
    pre_copy.wait()

    factor = PREFIX ** (-0.5) * math.log2(math.e)
    tile = 512
    side = pairs * chunk

    def prefix_of(j):
        t, c = half_of(j)
        return jnp.concatenate([part_of(x_bufs[0], t, c), part_of(x_bufs[1], t, c)], axis=1).astype(BF16)

    @pl.loop(0, 2)
    def _(h):
        @pl.when(h == 1)
        def _():
            x_step(3)

        @pl.loop(0, pairs)
        def _(t):
            j = h * pairs + t
            index(j, *half_of(j))

        @pl.when(h == 1)
        def _():
            idx_copy.start()
            send(sel_buf.at[pl.ds(pairs, pairs)], sel_got, ws.at[0], wr.at[0], sibling)

        q = jnp.concatenate([prefix_of(h * pairs + t) for t in range(pairs)], axis=0)
        most = jnp.full((side, LANES), -jnp.inf, F32)
        for u in range(r_dev // tile):
            s = lax.dot_general(
                q, pre_v[u * tile : (u + 1) * tile, :], NT, preferred_element_type=F32
            )
            logits[h, :, u * tile : (u + 1) * tile] = s
            for v in range(tile // LANES):
                most = jnp.maximum(most, s[:, v * LANES : (v + 1) * LANES])
        tops[h] = jnp.broadcast_to(jnp.max(most, axis=1, keepdims=True) * factor, (side, LANES))

    idx_copy.wait()
    rest_copy.wait()

    half = pairs * n_slot // QB

    @pl.loop(0, 2)
    def _(h):
        @pl.loop(0, half, unroll=4)
        def _(gg):
            g = (1 - h) * half + gg
            sub = lax.broadcasted_iota(jnp.int32, (QB, width), 0)
            rows = jnp.zeros((QB, width), F32)
            for k in range(QB):
                at = g * QB + k
                i = jnp.clip(idx_s[lax.div(at, n_slot), lax.rem(at, n_slot)], 0, r_dev - 1)
                group = slab_v[i >> 3].astype(F32)
                rows = jnp.where(sub == k, pltpu.roll(group, (k - (i & 7)) & 7, 0), rows)
            rows_buf[g] = rows.astype(BF16)

        @pl.when(h == 0)
        def _():
            send(rows_buf.at[pl.ds(half, half)], rows_got, ws.at[1], wr.at[1], sibling)

    @pl.loop(0, 2)
    def _(hh):
        h = 1 - hh
        top = tops[h][:, 0:1]
        total = jnp.zeros((side, LANES), F32)
        acc = jnp.zeros((side, PREFIX), F32)
        for u in range(r_dev // tile):
            w = jnp.exp2(logits[h, :, u * tile : (u + 1) * tile] * factor - top)
            for v in range(tile // LANES):
                total = total + w[:, v * LANES : (v + 1) * LANES]
            acc = acc + jnp.dot(
                w.astype(BF16), pre_v[u * tile : (u + 1) * tile, :], preferred_element_type=F32
            )
        total = jnp.sum(total, axis=1, keepdims=True)
        lane = lane_of(side)
        p0, p1 = acc[:, :LANES], acc[:, LANES:]
        b = jnp.where(lane < 32, pltpu.roll(p0, 32, 1), pltpu.roll(p1, 32, 1))
        c = jnp.where(lane < F_LANE, pltpu.roll(p1, 64, 1), 0.0)
        c = jnp.where(lane == L_LANE, total, c)
        for p, v in enumerate((p0, b, c)):
            pay[pl.ds(h * pairs, pairs), p] = jnp.where(lane == M_LANE, top, v).reshape((pairs,) + box)

        @pl.when(hh == 0)
        def _():
            for t in range(pairs):
                send(pay.at[pairs + t], got0.at[t], s0.at[t], r0.at[t], sibling)

    f_step(2)
    wait_bytes(sel_got, wr.at[0])
    wait_bytes(rows_got, wr.at[1])

    sibling_f = me_f + (1 - 2 * core).astype(F32)
    step = n_slot // QB

    @pl.loop(0, pairs, unroll=pairs)
    def _(t):
        def rows_of(lo, hi):
            groups = pl.ds(t * step, step)
            mine = rows_buf[groups, :, lo:hi].astype(F32).reshape(n_slot, hi - lo)
            other = rows_got[groups, :, lo:hi].astype(F32).reshape(n_slot, hi - lo)
            return jnp.concatenate([mine, other], axis=0).astype(BF16)

        scores = lax.dot_general(prefix_of(t), rows_of(0, PREFIX), NT, preferred_element_type=F32)
        for p in range(3):
            scores = scores + lax.dot_general(
                part_of(f_bufs[p], t).astype(BF16),
                rows_of(col0[p], col0[p + 1]),
                NT,
                preferred_element_type=F32,
            )
        lane = lane_of(chunk)
        numbers = jnp.where(lane < k_count, part_of(x_bufs[2], t, core), -1.0)
        full = jnp.sum(scores[:, :n_slot] * sel_buf[t], axis=1, keepdims=True)
        full2 = jnp.sum(scores[:, n_slot:] * sel_got[t], axis=1, keepdims=True)
        full = jnp.where(numbers == me_f, full, jnp.where(numbers == sibling_f, full2, 0.0))
        pay[t, 2] = pay[t, 2] + pltpu.roll(full, F_LANE, 1).reshape(box)

    def at_axis(axes, axis, index):
        return tuple(index if a == axis else slice(None) for a in axes)

    for p in range(3):

        @pl.loop(0, pairs, unroll=pairs)
        def _(t, p=p):
            if p == 0:
                wait_bytes(got0.at[t], r0.at[t])
            both = merge(p, [pay[t, p].reshape(chunk, LANES), got0[t, p].reshape(chunk, LANES)])
            mid0[p, pl.ds(2 * t, 2)] = both.reshape(box)

        axis = ORDERS[p][0]
        for k in far_first:
            to = peer(axis, k)
            send(mid0.at[(p,) + at_axis(range(3), axis, to[axis])], got1.at[p, k - 1], rs.at[0], rr.at[p], device(to, core))

    flat1 = (n * n * QB, LANES)
    for p in range(3):
        wait_bytes(got1.at[p], rr.at[p])
        first = ORDERS[p][0]
        own = mid0[(p,) + at_axis(range(3), first, coord[first])].reshape(flat1)
        blocks = [own] + [got1[p, k - 1].reshape(flat1) for k in range(1, n)]
        mid1[p] = merge(p, blocks).reshape(n, n, QB, LANES)
        left = [a for a in range(3) if a != first]
        for k in range(n * n - 1):
            k2, k3 = (k + 1) // n, (k + 1) % n
            to = peer(left[0], k2, left[1], k3)
            send(mid1.at[p, to[left[0]], to[left[1]]], got2.at[p, k], rs.at[1], rr.at[3 + p], device(to, core))

    out = []
    for p in range(3):
        wait_bytes(got2.at[p], rr.at[3 + p])
        left = [coord[a] for a in range(3) if a != ORDERS[p][0]]
        own = mid1[p, left[0], left[1]]
        out.append(merge(p, [own] + [got2[p, k] for k in range(n * n - 1)]))

    lane = lane_of(QB)
    a, b, c = out
    total = c[:, L_LANE : L_LANE + 1]
    b_back = pltpu.roll(b, 96, 1)
    out_ref[:, 0:LANES] = jnp.where(lane < 96, a, b_back) / total
    out_ref[:, LANES:PREFIX] = jnp.where(lane < 64, b_back, pltpu.roll(c, 64, 1)) / total
    lse = c[:, M_LANE:] * math.log(2.0) + jnp.log(total)
    full = pltpu.roll(c, LANES - F_LANE, 1) * width ** (-0.5)
    out_ref[:, PREFIX : PREFIX + LANES] = full - lse
    out_ref[:, PREFIX + LANES :] = jnp.broadcast_to(lse, (QB, LANES))

    for phase in range(4):
        wait_bytes(x_buf.at[(slice(None),) + phase_box(phase) + (0,)], xs.at[phase])
    for phase in range(3):
        for p in range(3):
            wait_bytes(f_bufs[p].at[phase_box(phase)], fs.at[p * 3 + phase])
    wait_bytes(sel_got, ws.at[0])
    wait_bytes(rows_got, ws.at[1])
    for t in range(pairs):
        wait_bytes(got0.at[t], s0.at[t])
    wait_bytes(got1, rs.at[0])
    wait_bytes(got2, rs.at[1])


def split(in_ref, pooled_ref, lse_ref, margin_ref):
    pooled_ref[...] = in_ref[:, 0:PREFIX]
    margin_ref[...] = in_ref[:, PREFIX : PREFIX + margin_ref.shape[1]]
    here = lax.broadcasted_iota(jnp.int32, (QB, LANES), 0) == lane_of(QB)
    lse = jnp.sum(jnp.where(here, in_ref[:, PREFIX + LANES :], 0.0), axis=0, keepdims=True)
    lse_ref[...] = lse[:, 0:QB]


def make(mesh, dims):
    def on_device(queries, slab, cand_owner, cand_row):
        width = queries.shape[1]
        r_dev = slab.shape[0]
        k_count = cand_owner.shape[1]
        tiles = (width - PREFIX) // LANES
        n0 = -(-tiles // 3)
        n1 = -(-(tiles - n0) // 2)
        col0 = (PREFIX, PREFIX + n0 * LANES, PREFIX + (n0 + n1) * LANES, width)
        n = dims[0]
        chunk = 2 * n * n * QB
        n_slot = chunk // QB * SLOTS
        vmem = pltpu.VMEM
        dma = pltpu.SemaphoreType.DMA
        spec = pl.BlockSpec(memory_space=pltpu.VMEM)
        merged = pl.pallas_call(
            functools.partial(kernel, dims, col0),
            out_shape=jax.ShapeDtypeStruct((QB, PREFIX + 2 * LANES), F32),
            in_specs=[spec, pl.BlockSpec(memory_space=pl.ANY), pl.BlockSpec(memory_space=pl.ANY), spec, spec],
            out_specs=spec,
            scratch_shapes=[
                vmem((r_dev, PREFIX), BF16),
                vmem((r_dev // QB, QB, width), BF16),
                vmem((3, n, n, n, 2, QB, LANES), BF16),
                vmem((n, n, n, QB, col0[1] - col0[0]), BF16),
                vmem((n, n, n, QB, col0[2] - col0[1]), BF16),
                vmem((n, n, n, QB, col0[3] - col0[2]), BF16),
                vmem((n, chunk, n_slot), F32),
                vmem((n // 2, chunk, n_slot), F32),
                vmem((QB, LANES), jnp.int32),
                pltpu.SMEM((QB, LANES), jnp.int32),
                vmem((n * n_slot // QB, QB, width), BF16),
                vmem((n * n_slot // QB // 2, QB, width), BF16),
                vmem((2, n // 2 * chunk, r_dev), F32),
                vmem((2, n // 2 * chunk, LANES), F32),
                vmem((n, 3) + (2, n, n, QB, LANES), F32),
                vmem((n // 2, 3) + (2, n, n, QB, LANES), F32),
                vmem((3, n, n, n, QB, LANES), F32),
                vmem((3, n - 1, n, n, QB, LANES), F32),
                vmem((3, n, n, QB, LANES), F32),
                vmem((3, n * n - 1, QB, LANES), F32),
                dma((3,)),
                dma((4,)),
                dma((12,)),
                dma((9,)),
                dma((9,)),
                dma((2,)),
                dma((2,)),
                dma((n // 2,)),
                dma((n // 2,)),
                dma((2,)),
                dma((6,)),
            ],
            compiler_params=pltpu.CompilerParams(
                collective_id=0, has_side_effects=True, vmem_limit_bytes=56 * 2**20
            ),
        )(queries, slab, slab.reshape(r_dev // QB, QB, width), cand_owner, cand_row)
        pooled, lse, margin = pl.pallas_call(
            split,
            out_shape=(
                jax.ShapeDtypeStruct((QB, PREFIX), F32),
                jax.ShapeDtypeStruct((1, QB), F32),
                jax.ShapeDtypeStruct((QB, k_count), F32),
            ),
            in_specs=[spec],
            out_specs=(spec, spec, spec),
        )(merged)
        return pooled, lse.reshape(QB), margin

    both = ("index", "query")
    return jax.shard_map(
        on_device,
        mesh=mesh,
        in_specs=(P(both, None),) * 4,
        out_specs=(P(both, None), P(both), P(both, None)),
        check_vma=False,
    )


def solution(mesh):
    side = math.isqrt(mesh.shape["index"])
    return make(mesh, (side, side, mesh.shape["query"] // 2))
```
